128 devices in a mesh: dap: 128 (over z, y, x, core).
Axes of the slice: x: 4, y: 4, z: 4, core: 2. Of those that a mesh axis runs over, the one named last changes fastest.
Arguments:
- pair: bfloat16 [512, 512, 128], P('dap'), may hold values from -6 to 6
- pair_mask: int32 [512, 512], P('dap'), may hold values 0 or 1
- norm_gains: float32 [3, 128], replicated, may hold values from 0.25 to 1.75
- w_edges: bfloat16 [128, 512], replicated, may hold values from -0.5 to 0.5
- w_tri_gate: bfloat16 [128, 128], replicated, may hold values from -0.5 to 0.5
- w_tri_out: bfloat16 [128, 128], replicated, may hold values from -0.5 to 0.5
- w_attn_in: bfloat16 [128, 512], replicated, may hold values from -0.5 to 0.5
- w_tri_bias: bfloat16 [128, 4], replicated, may hold values from -0.5 to 0.5
- w_attn_out: bfloat16 [128, 128], replicated, may hold values from -0.5 to 0.5
Outputs:
- updated: bfloat16 [512, 512, 128], P('dap')
The draws below stay inside these ranges and needn't reach their ends.
All inputs are finite; a program needn't handle non-finite values. No bound on the sum of `pair_mask` on one device may be relied on, other than what follows from the above.
Results may differ from the reference program's by a relative error of at most 0.013.
Values may be sent and summed in bfloat16 or wider, within the bound.
No kernel may reach another device: no remote copies, remote signals or barrier semaphores. Data moves between devices by JAX's collectives and lax.ppermute only.
A program may use at most 256 MiB of HBM per device.

```python
import jax
import jax.numpy as jnp
from jax import lax

C = 128
CH = 128
HEADS = 4
HEAD_DIM = 32
N_RES = 512


def place_ends(result, stream_key, smallest, top_value):
    longest = result.shape.index(max(result.shape))
    spots = []
    for shift in (0, 1):
        where = [jax.random.randint(jax.random.fold_in(stream_key, axis), (), 0, length) for axis, length in enumerate(result.shape)]
        where[longest] = (where[longest] + shift) % result.shape[longest]
        spots.append(tuple(where))
    return result.at[spots[0]].set(smallest).at[spots[1]].set(top_value)


def shard_levels(key, shape, pieces, least, largest):
    def one(axis_at, parts):
        steps = jax.random.uniform(jax.random.fold_in(jax.random.fold_in(key, 6), axis_at), (parts,), jnp.float32, least / len(pieces), largest / len(pieces))
        return jnp.repeat(jnp.exp(steps), shape[axis_at] // parts).reshape((-1,) + (1,) * (len(shape) - axis_at - 1))

    level = one(*pieces[0])
    for cut in pieces[1:]:
        level = level * one(*cut)
    return level


def centred(stream_key, dims, scale, bound, split=(), kind=jnp.bfloat16):
    factor_of = shard_levels(stream_key, dims, split, -0.22, 0.18) if split else 1.0
    result = jax.random.normal(stream_key, dims, jnp.float32) * scale * factor_of
    return jnp.minimum(jnp.maximum(result, -bound), bound).astype(kind)


def setup_inputs(seed: int = 0) -> dict:
    splits = jax.random.split(jax.random.key(seed), 10)
    pair = centred(splits[0], (N_RES, N_RES, C), 1.0, 6.0, ((0, 128),))
    pair_mask = place_ends((jax.random.randint(splits[1], (N_RES, N_RES), 0, 8) < 7).astype(jnp.int32), jax.random.fold_in(splits[1], 1), 0, 1)
    norm_gains = jnp.clip(1.0 + 0.15 * jax.random.normal(splits[2], (3, C), jnp.float32), 0.25, 1.75)
    w_edges = centred(splits[3], (C, 4 * CH), C ** -0.5, 0.5)
    w_tri_gate = centred(splits[4], (C, C), C ** -0.5, 0.5)
    w_tri_out = centred(splits[5], (CH, C), CH ** -0.5, 0.5)
    w_attn_in = centred(splits[6], (C, 4 * HEADS * HEAD_DIM), C ** -0.5, 0.5)
    w_tri_bias = centred(splits[7], (C, HEADS), C ** -0.5, 0.5)
    w_attn_out = centred(splits[8], (HEADS * HEAD_DIM, C), (HEADS * HEAD_DIM) ** -0.5, 0.5)
    return dict(pair=pair, pair_mask=pair_mask, norm_gains=norm_gains, w_edges=w_edges, w_tri_gate=w_tri_gate, w_tri_out=w_tri_out, w_attn_in=w_attn_in, w_tri_bias=w_tri_bias, w_attn_out=w_attn_out)


def layer_norm(values, gain):
    mean = lax.optimization_barrier(jnp.mean(values, axis=-1, keepdims=True))
    centered = values - mean
    var = lax.optimization_barrier(jnp.mean(centered * centered, axis=-1, keepdims=True))
    return centered / jnp.sqrt(var + 1e-05) * gain

def reference(pair, pair_mask, norm_gains, w_edges, w_tri_gate, w_tri_out, w_attn_in, w_tri_bias, w_attn_out):
    width = HEADS * HEAD_DIM
    pair_f = pair.astype(jnp.float32)
    normed = layer_norm(pair_f, norm_gains[0]).astype(jnp.bfloat16)
    edges = jnp.einsum('ijc,cd->ijd', normed.astype(jnp.float32), w_edges.astype(jnp.float32))
    mask_f = pair_mask.astype(jnp.float32)[:, :, None]
    left = (mask_f * jax.nn.sigmoid(edges[:, :, 0:CH]) * edges[:, :, CH:2 * CH]).astype(jnp.bfloat16)
    right = (mask_f * jax.nn.sigmoid(edges[:, :, 2 * CH:3 * CH]) * edges[:, :, 3 * CH:4 * CH]).astype(jnp.bfloat16)
    right_f = right.astype(jnp.float32)
    gate_w = w_tri_gate.astype(jnp.float32)
    out_w = w_tri_out.astype(jnp.float32)

    def tri_row(inputs):
        left_row, normed_row, pair_row = inputs
        product = jnp.einsum('kc,jkc->jc', left_row.astype(jnp.float32), right_f)
        prod_normed = layer_norm(product, norm_gains[1]).astype(jnp.bfloat16)
        gate = jax.nn.sigmoid(jnp.dot(normed_row.astype(jnp.float32), gate_w))
        update = gate * jnp.dot(prod_normed.astype(jnp.float32), out_w)
        return (pair_row + update).astype(jnp.bfloat16)
    pair_mid = lax.map(tri_row, (left, normed, pair_f))
    mid_f = pair_mid.astype(jnp.float32)
    mid_normed = layer_norm(mid_f, norm_gains[2]).astype(jnp.bfloat16)
    tri_bias = jnp.einsum('jkc,ch->hjk', mid_normed.astype(jnp.float32), w_tri_bias.astype(jnp.float32)).astype(jnp.bfloat16)
    bias_f = tri_bias.astype(jnp.float32)
    in_w = w_attn_in.astype(jnp.float32)
    attn_w = w_attn_out.astype(jnp.float32)
    total = mid_normed.shape[0]

    def attn_row(inputs):
        normed_row, mask_row, mid_row = inputs
        packed = jnp.dot(normed_row.astype(jnp.float32), in_w)
        query = packed[:, 0:width].astype(jnp.bfloat16).astype(jnp.float32).reshape(total, HEADS, HEAD_DIM)
        key = packed[:, width:2 * width].astype(jnp.bfloat16).astype(jnp.float32).reshape(total, HEADS, HEAD_DIM)
        value = packed[:, 2 * width:3 * width].astype(jnp.bfloat16).astype(jnp.float32).reshape(total, HEADS, HEAD_DIM)
        att_gate = jax.nn.sigmoid(packed[:, 3 * width:4 * width])
        logits = jnp.einsum('jhd,khd->hjk', query, key) / jnp.sqrt(jnp.float32(HEAD_DIM))
        logits = logits + bias_f + 1000000000.0 * (mask_row.astype(jnp.float32)[None, None, :] - 1.0)
        top = lax.optimization_barrier(jnp.max(logits, axis=-1, keepdims=True))
        expo = jnp.exp(logits - top)
        weights = (expo / lax.optimization_barrier(jnp.sum(expo, axis=-1, keepdims=True))).astype(jnp.bfloat16)
        mixed = jnp.einsum('hjk,khd->jhd', weights.astype(jnp.float32), value).reshape(total, width)
        attended = (att_gate * mixed).astype(jnp.bfloat16)
        return (mid_row + jnp.dot(attended.astype(jnp.float32), attn_w)).astype(jnp.bfloat16)
    return lax.map(attn_row, (mid_normed, pair_mask, mid_f))
```

```python
import functools
import math

import jax
import jax.numpy as jnp
from jax import lax
from jax.experimental import pallas as pl
from jax.experimental.pallas import tpu as pltpu
from jax.sharding import PartitionSpec as P

F32 = jnp.float32
BF16 = jnp.bfloat16
VMEM_LIMIT = 48 * 1024 * 1024
LOG2E = math.log2(math.e)


def dot(a, b, ca, cb):
    return lax.dot_general(a, b, (((ca,), (cb,)), ((), ())), preferred_element_type=F32)


def norm_rows(values, gain):
    mean = jnp.mean(values, axis=-1, keepdims=True)
    centered = values - mean
    var = jnp.mean(centered * centered, axis=-1, keepdims=True)
    return centered * lax.rsqrt(var + 1e-05) * gain


def edges_kernel(pair_ref, mask_ref, gains_ref, w_ref, out_ref):
    row = pl.program_id(0)
    hidden = out_ref.shape[0]
    normed = norm_rows(pair_ref[...].astype(F32), gains_ref[0:1, :]).astype(BF16)
    edges = dot(w_ref[...], normed, 0, 1)
    mask = mask_ref[pl.ds(row, 1), :].astype(F32)
    for side in range(2):
        gate = edges[2 * side * hidden : (2 * side + 1) * hidden]
        value = edges[(2 * side + 1) * hidden : (2 * side + 2) * hidden]
        out_ref[:, side, :] = (mask * jax.nn.sigmoid(gate) * value).astype(BF16)


def product_kernel(left_ref, right_ref, out_ref):
    total = right_ref.shape[0]
    for row in range(left_ref.shape[1] // total):
        cols = slice(row * total, (row + 1) * total)
        out_ref[:, cols] = dot(left_ref[:, cols], right_ref[...], 1, 1).astype(BF16)


def middle_kernel(prod_ref, pair_ref, gains_ref, wg_ref, wo_ref, wb_ref, mid_ref, normed_ref, bias_ref):
    prod = prod_ref[...].astype(F32)
    mean = jnp.mean(prod, axis=0, keepdims=True)
    centered = prod - mean
    var = jnp.mean(centered * centered, axis=0, keepdims=True)
    prod_normed = (centered * lax.rsqrt(var + 1e-05) * gains_ref[1:2, :].T).astype(BF16)
    pair = pair_ref[...].astype(F32)
    normed = norm_rows(pair, gains_ref[0:1, :]).astype(BF16)
    gate = jax.nn.sigmoid(dot(normed, wg_ref[...], 1, 0))
    mid = (pair + gate * dot(prod_normed, wo_ref[...], 0, 0)).astype(BF16)
    mid_ref[...] = mid
    mid_normed = norm_rows(mid.astype(F32), gains_ref[2:3, :]).astype(BF16)
    normed_ref[...] = mid_normed
    bias_ref[...] = dot(wb_ref[...], mid_normed, 0, 1).astype(BF16)


def attention_kernel(head_dim, normed_ref, mid_ref, mask_ref, bias_ref, win_ref, wout_ref, out_ref):
    row = pl.program_id(0)
    heads = bias_ref.shape[0]
    total, width = normed_ref.shape
    packed = dot(normed_ref[...], win_ref[...], 1, 0)
    query = packed[:, 0:width].astype(BF16)
    key = packed[:, width : 2 * width].astype(BF16)
    value = packed[:, 2 * width : 3 * width].astype(BF16)
    lane_head = lax.broadcasted_iota(jnp.int32, (1, width), 1) // head_dim
    mask = 1000000000.0 * (mask_ref[pl.ds(row, 1), :].astype(F32) - 1.0)
    scale = 1.0 / math.sqrt(head_dim)
    mixed = jnp.zeros((total, 2 * width), F32)
    for head in range(heads):
        pick = (lane_head == head).astype(BF16)
        logits = dot(query * pick, key, 1, 1) * scale + bias_ref[head].astype(F32) + mask
        top = jnp.max(logits, axis=-1, keepdims=True)
        expo = jnp.exp(logits - top).astype(BF16)
        both = jnp.concatenate([value * pick, jnp.broadcast_to(pick, value.shape)], axis=1)
        mixed = mixed + dot(expo, both, 1, 0)
    att_gate = jax.nn.sigmoid(packed[:, 3 * width : 4 * width])
    attended = (att_gate * mixed[:, :width] / mixed[:, width:]).astype(BF16)
    update = dot(attended, wout_ref[...], 1, 0)
    out_ref[...] = (mid_ref[...].astype(F32) + update).astype(BF16)


def params():
    return pltpu.CompilerParams(vmem_limit_bytes=VMEM_LIMIT)


def whole(array):
    return pl.BlockSpec(array.shape, lambda *_: (0,) * array.ndim)


def exchange(array):
    return lax.all_to_all(array, "dap", 0, 0, tiled=True)


def per_device(
    pair, pair_mask, norm_gains, w_edges, w_tri_gate, w_tri_out, w_attn_in, w_tri_bias, w_attn_out
):
    rows, total, width = pair.shape
    hidden = w_tri_out.shape[0]
    heads = w_tri_bias.shape[1]
    devices = total // rows
    flat = pair.reshape(rows * total, width)
    row_block = pl.BlockSpec((total, width), lambda r: (r, 0))
    sides = pl.pallas_call(
        edges_kernel,
        grid=(rows,),
        in_specs=[row_block, whole(pair_mask), whole(norm_gains), whole(w_edges)],
        out_specs=pl.BlockSpec((hidden, 2, total), lambda r: (0, 0, r)),
        out_shape=jax.ShapeDtypeStruct((hidden, 2, rows * total), BF16),
        compiler_params=params(),
    )(flat, pair_mask, norm_gains, w_edges)
    sides = exchange(sides)
    left = sides[:, 0]
    right = sides[:, 1].reshape(total, total)
    product = pl.pallas_call(
        product_kernel,
        out_shape=jax.ShapeDtypeStruct((devices, rows * total), BF16),
        compiler_params=params(),
    )(left, right)
    product = exchange(product)
    mid, mid_normed, bias = pl.pallas_call(
        middle_kernel,
        grid=(rows,),
        in_specs=[
            pl.BlockSpec((hidden, total), lambda r: (0, r)),
            row_block,
            whole(norm_gains),
            whole(w_tri_gate),
            whole(w_tri_out),
            whole(w_tri_bias),
        ],
        out_specs=[row_block, row_block, pl.BlockSpec((heads, total), lambda r: (0, r))],
        out_shape=[
            jax.ShapeDtypeStruct((rows * total, width), BF16),
            jax.ShapeDtypeStruct((rows * total, width), BF16),
            jax.ShapeDtypeStruct((heads, rows * total), BF16),
        ],
        compiler_params=params(),
    )(product, flat, norm_gains, w_tri_gate, w_tri_out, w_tri_bias)
    bias = exchange(jnp.broadcast_to(bias.reshape(1, heads, rows, total), (devices, heads, rows, total)))
    bias = bias.transpose(1, 0, 2, 3).reshape(heads, total, total)
    updated = pl.pallas_call(
        functools.partial(attention_kernel, width // heads),
        grid=(rows,),
        in_specs=[
            row_block,
            row_block,
            whole(pair_mask),
            whole(bias),
            whole(w_attn_in),
            whole(w_attn_out),
        ],
        out_specs=row_block,
        out_shape=jax.ShapeDtypeStruct((rows * total, width), BF16),
        compiler_params=params(),
    )(mid_normed, mid, pair_mask, bias, w_attn_in, w_attn_out)
    return updated.reshape(rows, total, width)


def solution(mesh):
    placed = (P("dap", None, None), P("dap", None), P(), P(), P(), P(), P(), P(), P())
    return jax.shard_map(
        per_device, mesh=mesh, in_specs=placed, out_specs=P("dap", None, None), check_vma=False
    )
```

```python
import functools
import math

import jax
import jax.numpy as jnp
from jax import lax
from jax.experimental import pallas as pl
from jax.experimental.pallas import tpu as pltpu
from jax.sharding import PartitionSpec as P

F32 = jnp.float32
BF16 = jnp.bfloat16
VMEM_LIMIT = 40 * 1024 * 1024
LOG2E = math.log2(math.e)
TILE = 8


def dot(a, b, ca, cb):
    return lax.dot_general(a, b, (((ca,), (cb,)), ((), ())), preferred_element_type=F32)


def sigmoid(x):
    return 0.5 + 0.5 * jnp.tanh(0.5 * x)


def norm_rows(values, gain):
    mean = jnp.mean(values, axis=-1, keepdims=True)
    centered = values - mean
    var = jnp.mean(centered * centered, axis=-1, keepdims=True)
    return centered * lax.rsqrt(var + 1e-05) * gain


def put_rows(scratch, start, stride, values):
    for lane in range(values.shape[1] // 128):
        scratch[lane, pl.ds(start, values.shape[0], stride=stride), :] = values[:, lane * 128 : (lane + 1) * 128]


def get_rows(scratch, start, size, stride):
    return jnp.concatenate(
        [scratch[lane, pl.ds(start, size, stride=stride), :] for lane in range(scratch.shape[0])], axis=1
    )


def spill(scratch, values):
    for lane in range(scratch.shape[0]):
        part = values[:, :, lane * 128 : (lane + 1) * 128].astype(F32)
        scratch[lane] = part.reshape(scratch.shape[1], 128)


def fill(out_ref, scratch):
    for lane in range(scratch.shape[0]):
        part = scratch[lane].reshape(out_ref.shape[0], TILE, 128)
        out_ref[:, :, lane * 128 : (lane + 1) * 128] = part.astype(BF16)


def edges_kernel(pair_ref, mask_ref, gains_ref, w_ref, out_ref, scratch):
    rows, total = mask_ref.shape
    hidden = out_ref.shape[0]
    for row in range(rows):
        pair = pair_ref[row].astype(F32)
        normed = norm_rows(pair, gains_ref[0:1, :]).astype(BF16)
        edges = dot(w_ref[...], normed, 0, 1)
        mask = mask_ref[row : row + 1, :].astype(F32)
        for side in range(2):
            gate = edges[2 * side * hidden : (2 * side + 1) * hidden]
            value = edges[(2 * side + 1) * hidden : (2 * side + 2) * hidden]
            put_rows(scratch, side * rows + row, TILE, mask * sigmoid(gate) * value)
    fill(out_ref, scratch)


def product_kernel(sides_ref, out_ref, scratch, right_ref, prod_ref):
    devices, _, total = sides_ref.shape
    rows = total // devices
    half = total // 2
    spill(scratch, sides_ref[...])
    for row in range(rows):
        put_rows(right_ref, row, rows, get_rows(scratch, rows + row, devices, TILE))
    right = jnp.concatenate([right_ref[lane] for lane in range(total // 128)], axis=1).astype(BF16)
    for row in range(rows):
        left = get_rows(scratch, row, devices, TILE).astype(BF16)
        product = dot(left, right, 1, 1)
        for part in range(2):
            put_rows(prod_ref, 2 * row + part, TILE, product[:, part * half : (part + 1) * half])
    fill(out_ref, prod_ref)


def middle_kernel(
    prod_ref, pair_ref, gains_ref, wg_ref, wo_ref, wb_ref, mid_ref, normed_ref, bias_ref, scratch, bias_f
):
    rows, total, width = pair_ref.shape
    heads = wb_ref.shape[1]
    devices = bias_ref.shape[0]
    spill(scratch, prod_ref[...])
    gain = gains_ref[1:2, :].T
    for row in range(rows):
        prod = jnp.concatenate(
            [get_rows(scratch, 2 * row + part, width, TILE) for part in range(2)], axis=1
        )
        mean = jnp.mean(prod, axis=0, keepdims=True)
        centered = prod - mean
        var = jnp.mean(centered * centered, axis=0, keepdims=True)
        prod_normed = (centered * lax.rsqrt(var + 1e-05) * gain).astype(BF16)
        pair = pair_ref[row].astype(F32)
        normed = norm_rows(pair, gains_ref[0:1, :]).astype(BF16)
        gate = sigmoid(dot(normed, wg_ref[...], 1, 0))
        mid = (pair + gate * dot(prod_normed, wo_ref[...], 0, 0)).astype(BF16)
        mid_ref[row] = mid
        mid_normed = norm_rows(mid.astype(F32), gains_ref[2:3, :]).astype(BF16)
        normed_ref[row] = mid_normed
        bias = dot(wb_ref[...], mid_normed, 0, 1)
        for head in range(heads):
            bias_f[head * rows + row : head * rows + row + 1, :] = bias[head : head + 1, :]
    for part in range(2):
        block = bias_f[part * TILE : (part + 1) * TILE, :].astype(BF16)
        for pair_of in range(devices // 2):
            bias_ref[2 * pair_of + part] = block


def attention_kernel(
    head_dim, last, first_head, normed_ref, mask_ref, bias_ref, win_ref, *rest
):
    if last:
        mid_ref, part_ref, wout_ref, out_ref, scratch, bias_f = rest
    else:
        out_ref, scratch, bias_f = rest
    rows, total, width = normed_ref.shape
    devices = bias_ref.shape[0]
    own = TILE // rows
    spill(scratch, bias_ref[...])
    for head in range(own):
        for row in range(rows):
            values = get_rows(scratch, head * rows + row, devices, TILE) * LOG2E
            put_rows(bias_f.at[head], row, rows, values)
    base = first_head[0]
    lane_head = lax.broadcasted_iota(jnp.int32, (1, width), 1) // head_dim
    scale = LOG2E / math.sqrt(head_dim)
    for row in range(rows):
        packed = dot(normed_ref[row], win_ref[...], 1, 0)
        query = (packed[:, 0:width] * scale).astype(BF16)
        key = packed[:, width : 2 * width].astype(BF16)
        value = packed[:, 2 * width : 3 * width].astype(BF16)
        mask = (1000000000.0 * LOG2E) * (mask_ref[row : row + 1, :].astype(F32) - 1.0)
        mixed = jnp.zeros((total, 2 * width), F32)
        for head in range(own):
            pick = (lane_head == base + head).astype(BF16)
            bias = jnp.concatenate([bias_f[head, lane] for lane in range(total // 128)], axis=1)
            logits = dot(query * pick, key, 1, 1) + bias + mask
            top = jnp.max(logits, axis=-1, keepdims=True)
            expo = jnp.exp2(logits - top).astype(BF16)
            both = jnp.concatenate([value * pick, jnp.broadcast_to(pick, value.shape)], axis=1)
            mixed = mixed + dot(expo, both, 1, 0)
        mine = (lane_head >= base) & (lane_head < base + own)
        share = jnp.where(mine, mixed[:, :width] / mixed[:, width:], 0.0)
        if last:
            att_gate = sigmoid(packed[:, 3 * width : 4 * width])
            attended = (att_gate * (share + part_ref[row])).astype(BF16)
            update = dot(attended, wout_ref[...], 1, 0)
            out_ref[row] = (mid_ref[row].astype(F32) + update).astype(BF16)
        else:
            out_ref[row] = share


def params():
    return pltpu.CompilerParams(vmem_limit_bytes=VMEM_LIMIT)


def call(kernel, out_shape, scratch, n_args, scalar_at=None):
    specs = [
        pl.BlockSpec(memory_space=pltpu.SMEM if at == scalar_at else pltpu.VMEM) for at in range(n_args)
    ]
    return pl.pallas_call(
        kernel,
        in_specs=specs,
        out_specs=jax.tree.map(lambda _: pl.BlockSpec(memory_space=pltpu.VMEM), out_shape),
        out_shape=out_shape,
        scratch_shapes=scratch,
        compiler_params=params(),
    )


def exchange(array):
    return lax.all_to_all(array, "dap", 0, 0, tiled=True)


def per_device(
    pair, pair_mask, norm_gains, w_edges, w_tri_gate, w_tri_out, w_attn_in, w_tri_bias, w_attn_out
):
    rows, total, width = pair.shape
    hidden = w_tri_out.shape[0]
    heads = w_tri_bias.shape[1]
    devices = total // rows
    lanes = total // 128
    shape = jax.ShapeDtypeStruct
    tall = pltpu.VMEM((lanes, devices * TILE, 128), F32)
    square = pltpu.VMEM((lanes, total, 128), F32)
    short = pltpu.VMEM((lanes // 2, devices * TILE, 128), F32)
    sides = call(edges_kernel, shape((hidden, TILE, total), BF16), [tall], 4)(
        pair, pair_mask, norm_gains, w_edges
    )
    sides = exchange(sides)
    product = call(
        product_kernel, shape((devices, TILE, total // 2), BF16), [tall, square, short], 1
    )(sides)
    product = exchange(product)
    mid, mid_normed, bias = call(
        middle_kernel,
        [
            shape((rows, total, width), BF16),
            shape((rows, total, width), BF16),
            shape((devices, TILE, total), BF16),
        ],
        [short, pltpu.VMEM((2 * TILE, total), F32)],
        6,
    )(product, pair, norm_gains, w_tri_gate, w_tri_out, w_tri_bias)
    mine = exchange(bias)
    swap = [(d, d ^ 1) for d in range(devices)]
    other = lax.ppermute(mine, "dap", swap)
    own = heads // 2
    core = lax.rem(lax.axis_index("dap"), 2)
    scratch = [tall, pltpu.VMEM((own, lanes, total, 128), F32)]
    part = call(
        functools.partial(attention_kernel, width // heads, False),
        shape((rows, total, width), F32),
        scratch,
        5,
        0,
    )(jnp.reshape(core * own, (1,)), mid_normed, pair_mask, mine, w_attn_in)
    return call(
        functools.partial(attention_kernel, width // heads, True),
        shape((rows, total, width), BF16),
        scratch,
        8,
        0,
    )(
        jnp.reshape((1 - core) * own, (1,)),
        mid_normed,
        pair_mask,
        other,
        w_attn_in,
        mid,
        part,
        w_attn_out,
    )


def solution(mesh):
    placed = (P("dap", None, None), P("dap", None), P(), P(), P(), P(), P(), P(), P())
    return jax.shard_map(
        per_device, mesh=mesh, in_specs=placed, out_specs=P("dap", None, None), check_vma=False
    )
```

```python
import functools
import math

import jax
import jax.numpy as jnp
from jax import lax
from jax.experimental import pallas as pl
from jax.experimental.pallas import tpu as pltpu
from jax.sharding import PartitionSpec as P

F32 = jnp.float32
BF16 = jnp.bfloat16
VMEM_LIMIT = 40 * 1024 * 1024
EDGES_LIMIT = 60 * 1024 * 1024
LOG2E = math.log2(math.e)
TILE = 8


def dot(a, b, ca, cb):
    return lax.dot_general(a, b, (((ca,), (cb,)), ((), ())), preferred_element_type=F32)


def sigmoid(x):
    return 0.5 + 0.5 * jnp.tanh(0.5 * x)


def norm_rows(values, gain):
    mean = jnp.mean(values, axis=-1, keepdims=True)
    centered = values - mean
    var = jnp.mean(centered * centered, axis=-1, keepdims=True)
    return centered * lax.rsqrt(var + 1e-05) * gain


def put_rows(scratch, start, stride, values):
    for lane in range(values.shape[1] // 128):
        scratch[lane, pl.ds(start, values.shape[0], stride=stride), :] = values[:, lane * 128 : (lane + 1) * 128]


def get_rows(scratch, start, size, stride):
    return jnp.concatenate(
        [scratch[lane, pl.ds(start, size, stride=stride), :] for lane in range(scratch.shape[0])], axis=1
    )


def spill(scratch, values):
    for lane in range(scratch.shape[0]):
        part = values[:, :, lane * 128 : (lane + 1) * 128].astype(F32)
        scratch[lane] = part.reshape(scratch.shape[1], 128)


def fill(out_ref, scratch):
    for lane in range(scratch.shape[0]):
        part = scratch[lane].reshape(out_ref.shape[0], TILE, 128)
        out_ref[:, :, lane * 128 : (lane + 1) * 128] = part.astype(BF16)


def edges_kernel(pair_ref, mask_ref, gains_ref, w_ref, out_ref, scratch):
    rows, total = mask_ref.shape
    hidden = out_ref.shape[0]
    normed = [norm_rows(pair_ref[row].astype(F32), gains_ref[0:1, :]).astype(BF16) for row in range(rows)]
    edges = [dot(w_ref[...], normed[row], 0, 1) for row in range(rows)]
    for row in range(rows):
        mask = mask_ref[row : row + 1, :].astype(F32)
        for side in range(2):
            gate = edges[row][2 * side * hidden : (2 * side + 1) * hidden]
            value = edges[row][(2 * side + 1) * hidden : (2 * side + 2) * hidden]
            put_rows(scratch, side * rows + row, TILE, mask * sigmoid(gate) * value)
    fill(out_ref, scratch)


def product_kernel(sides_ref, out_ref, scratch, right_ref, prod_ref):
    devices, _, total = sides_ref.shape
    rows = total // devices
    half = total // 2
    spill(scratch, sides_ref[...])
    for row in range(rows):
        put_rows(right_ref, row, rows, get_rows(scratch, rows + row, devices, TILE))
    right = jnp.concatenate([right_ref[lane] for lane in range(total // 128)], axis=1).astype(BF16)
    left = [get_rows(scratch, row, devices, TILE).astype(BF16) for row in range(rows)]
    product = [dot(left[row], right, 1, 1) for row in range(rows)]
    for row in range(rows):
        for part in range(2):
            put_rows(prod_ref, 2 * row + part, TILE, product[row][:, part * half : (part + 1) * half])
    fill(out_ref, prod_ref)


def gate_kernel(pair_ref, gains_ref, wg_ref, out_ref):
    for row in range(pair_ref.shape[0]):
        normed = norm_rows(pair_ref[row].astype(F32), gains_ref[0:1, :]).astype(BF16)
        out_ref[row] = sigmoid(dot(normed, wg_ref[...], 1, 0))


def middle_kernel(
    prod_ref,
    pair_ref,
    gate_ref,
    gains_ref,
    mask_ref,
    wo_ref,
    wb_ref,
    mid_ref,
    normed_ref,
    masked_ref,
    bias_ref,
    scratch,
    bias_f,
):
    rows, total, width = pair_ref.shape
    heads = wb_ref.shape[0]
    devices = bias_ref.shape[0]
    spill(scratch, prod_ref[...])
    gain = gains_ref[1:2, :].T
    masked_ref[...] = (1000000000.0 * LOG2E) * (mask_ref[...].astype(F32) - 1.0)
    prod_normed = []
    for row in range(rows):
        prod = jnp.concatenate(
            [get_rows(scratch, 2 * row + part, width, TILE) for part in range(2)], axis=1
        )
        mean = jnp.mean(prod, axis=0, keepdims=True)
        centered = prod - mean
        var = jnp.mean(centered * centered, axis=0, keepdims=True)
        prod_normed.append((centered * lax.rsqrt(var + 1e-05) * gain).astype(BF16))
    update = [dot(prod_normed[row], wo_ref[...], 0, 0) for row in range(rows)]
    mid = [(pair_ref[row].astype(F32) + gate_ref[row] * update[row]).astype(BF16) for row in range(rows)]
    mid_normed = []
    for row in range(rows):
        mid_ref[row] = mid[row]
        mid_normed.append(norm_rows(mid[row].astype(F32), gains_ref[2:3, :]).astype(BF16))
        normed_ref[row] = mid_normed[row]
    bias = [dot(wb_ref[...], mid_normed[row], 1, 1) for row in range(rows)]
    for row in range(rows):
        for head in range(heads):
            bias_f[head * rows + row : head * rows + row + 1, :] = bias[row][head : head + 1, :]
    for part in range(2):
        block = bias_f[part * TILE : (part + 1) * TILE, :].astype(BF16)
        for pair_of in range(devices // 2):
            bias_ref[2 * pair_of + part] = block


def attend(head_dim, first_head, query_ref, key_ref, value_ref, gate_ref, bias_ref, masked_ref, scratch, bias_f):
    rows, total, width = value_ref.shape
    devices = bias_ref.shape[0]
    own = TILE // rows
    spill(scratch, bias_ref[...])
    for head in range(own):
        for row in range(rows):
            values = get_rows(scratch, head * rows + row, devices, TILE) * LOG2E
            put_rows(bias_f.at[head], row, rows, values)
    base = first_head[0]
    lane_head = lax.broadcasted_iota(jnp.int32, (1, width), 1) // head_dim
    mine = (lane_head >= base) & (lane_head < base + own)
    attended = []
    for row in range(rows):
        expos, boths = [], []
        for head in range(own):
            pick = (lane_head == base + head).astype(BF16)
            bias = jnp.concatenate([bias_f[head, lane] for lane in range(total // 128)], axis=1)
            logits = dot(query_ref[row] * pick, key_ref[row], 1, 1) + bias + masked_ref[row : row + 1, :]
            top = jnp.max(logits, axis=-1, keepdims=True)
            expos.append(jnp.exp2(logits - top).astype(BF16))
            value = value_ref[row]
            boths.append(
                jnp.concatenate([value * pick, jnp.broadcast_to(pick, value.shape)], axis=1)
            )
        mixed = dot(jnp.concatenate(expos, axis=1), jnp.concatenate(boths, axis=0), 1, 0)
        share = jnp.where(mine, mixed[:, :width] / mixed[:, width:], 0.0)
        attended.append((gate_ref[row] * share).astype(BF16))
    return attended


def own_heads_kernel(
    head_dim,
    first_head,
    normed_ref,
    bias_ref,
    masked_ref,
    win_ref,
    query_ref,
    key_ref,
    value_ref,
    gate_ref,
    out_ref,
    scratch,
    bias_f,
):
    rows, total, width = normed_ref.shape
    scale = LOG2E / math.sqrt(head_dim)
    packed = [dot(normed_ref[row], win_ref[...], 1, 0) for row in range(rows)]
    for row in range(rows):
        query_ref[row] = (packed[row][:, 0:width] * scale).astype(BF16)
        key_ref[row] = packed[row][:, width : 2 * width].astype(BF16)
        value_ref[row] = packed[row][:, 2 * width : 3 * width].astype(BF16)
        gate_ref[row] = sigmoid(packed[row][:, 3 * width : 4 * width])
    attended = attend(
        head_dim, first_head, query_ref, key_ref, value_ref, gate_ref, bias_ref, masked_ref, scratch, bias_f
    )
    for row in range(rows):
        out_ref[row] = attended[row]


def other_heads_kernel(
    head_dim,
    first_head,
    query_ref,
    key_ref,
    value_ref,
    gate_ref,
    bias_ref,
    masked_ref,
    mid_ref,
    part_ref,
    wout_ref,
    out_ref,
    scratch,
    bias_f,
    result,
    sems,
):
    rows = mid_ref.shape[0]
    attended = attend(
        head_dim, first_head, query_ref, key_ref, value_ref, gate_ref, bias_ref, masked_ref, scratch, bias_f
    )
    copies = []
    for row in range(rows):
        update = dot(attended[row] + part_ref[row], wout_ref[...], 1, 0)
        result[row] = (mid_ref[row].astype(F32) + update).astype(BF16)
        copies.append(pltpu.make_async_copy(result.at[row], out_ref.at[row], sems.at[row]))
        copies[row].start()
    for copy in copies:
        copy.wait()


def call(kernel, out_shape, scratch, n_args, scalars=0, limit=VMEM_LIMIT, out_space=pltpu.VMEM, cost=None):
    specs = [
        pl.BlockSpec(memory_space=pltpu.SMEM if at < scalars else pltpu.VMEM) for at in range(n_args)
    ]
    return pl.pallas_call(
        kernel,
        in_specs=specs,
        out_specs=jax.tree.map(lambda _: pl.BlockSpec(memory_space=out_space), out_shape),
        out_shape=out_shape,
        scratch_shapes=scratch,
        compiler_params=pltpu.CompilerParams(vmem_limit_bytes=limit),
        cost_estimate=cost,
    )


def cost(flops, bytes_accessed, transcendentals):
    return pl.CostEstimate(
        flops=flops, bytes_accessed=bytes_accessed, transcendentals=transcendentals
    )


def exchange(array):
    return lax.all_to_all(array, "dap", 0, 0, tiled=True)


def per_device(
    pair, pair_mask, norm_gains, w_edges, w_tri_gate, w_tri_out, w_attn_in, w_tri_bias, w_attn_out
):
    rows, total, width = pair.shape
    hidden = w_tri_out.shape[0]
    heads = w_tri_bias.shape[1]
    head_dim = width // heads
    own = heads // 2
    devices = total // rows
    lanes = total // 128
    shape = jax.ShapeDtypeStruct
    tall = pltpu.VMEM((lanes, devices * TILE, 128), F32)
    square = pltpu.VMEM((lanes, total, 128), F32)
    short = pltpu.VMEM((lanes // 2, devices * TILE, 128), F32)
    sides = call(
        edges_kernel, shape((hidden, TILE, total), BF16), [tall], 4, limit=EDGES_LIMIT
    )(pair, pair_mask, norm_gains, w_edges)
    sides = exchange(sides)
    product = call(
        product_kernel, shape((devices, TILE, total // 2), BF16), [tall, square, short], 1
    )(sides)
    product = exchange(product)
    gate = call(
        gate_kernel,
        shape((rows, total, width), F32),
        [],
        3,
        cost=cost(2 * rows * total * width * width, 4 << 20, rows * total * width),
    )(pair, norm_gains, w_tri_gate)
    like = shape((rows, total, width), BF16)
    wide = shape((rows, total, width), F32)
    mid, mid_normed, masked, bias = call(
        middle_kernel,
        [like, like, shape((rows, total), F32), shape((devices, TILE, total), BF16)],
        [short, pltpu.VMEM((2 * TILE, total), F32)],
        7,
    )(product, pair, gate, norm_gains, pair_mask, w_tri_out, w_tri_bias.T)
    mine = exchange(bias)
    swap = [(d, d ^ 1) for d in range(devices)]
    other = lax.ppermute(mine, "dap", swap)
    core = lax.rem(lax.axis_index("dap"), 2)
    mine_first = jnp.reshape(core * own, (1,))
    other_first = jnp.reshape((1 - core) * own, (1,))
    scratch = [tall, pltpu.VMEM((own, lanes, total, 128), F32)]
    query, key, value, att_gate, part = call(
        functools.partial(own_heads_kernel, head_dim),
        [like, like, like, wide, like],
        scratch,
        5,
        1,
    )(mine_first, mid_normed, mine, masked, w_attn_in)
    scratch = scratch + [pltpu.VMEM((rows, total, width), BF16), pltpu.SemaphoreType.DMA((rows,))]
    return call(
        functools.partial(other_heads_kernel, head_dim),
        like,
        scratch,
        10,
        1,
        out_space=pl.ANY,
    )(other_first, query, key, value, att_gate, other, masked, mid, part, w_attn_out)


def solution(mesh):
    placed = (P("dap", None, None), P("dap", None), P(), P(), P(), P(), P(), P(), P())
    return jax.shard_map(
        per_device, mesh=mesh, in_specs=placed, out_specs=P("dap", None, None), check_vma=False
    )
```

```python
import functools
import math

import jax
import jax.numpy as jnp
from jax import lax
from jax.experimental import pallas as pl
from jax.experimental.pallas import tpu as pltpu
from jax.sharding import PartitionSpec as P

F32 = jnp.float32
BF16 = jnp.bfloat16
VMEM_LIMIT = 40 * 1024 * 1024
EDGES_LIMIT = 60 * 1024 * 1024
LOG2E = math.log2(math.e)
TILE = 8
MASK_AT, GAIN_AT, BIAS_AT, SMALL = 0, 8, 16, 24


def dot(a, b, ca, cb):
    return lax.dot_general(a, b, (((ca,), (cb,)), ((), ())), preferred_element_type=F32)


def sigmoid(x):
    return 0.5 + 0.5 * jnp.tanh(0.5 * x)


def norm_rows(values, gain):
    size = values.shape[-1]
    row = lax.broadcasted_iota(jnp.int32, (size, size), 0)
    col = lax.broadcasted_iota(jnp.int32, (size, size), 1)
    centering = ((row == col).astype(F32) - 1.0 / size).astype(BF16)
    average = jnp.full((size, size), 1.0 / size, BF16)
    centered = dot(values, centering, 1, 0)
    var = dot((centered * centered).astype(BF16), average, 1, 0)
    return (centered * lax.rsqrt(var + 1e-05) * gain).astype(BF16)


def put_rows(scratch, start, stride, values):
    for lane in range(values.shape[1] // 128):
        scratch[lane, pl.ds(start, values.shape[0], stride=stride), :] = values[:, lane * 128 : (lane + 1) * 128]


def get_rows(scratch, start, size, stride):
    return jnp.concatenate(
        [scratch[lane, pl.ds(start, size, stride=stride), :] for lane in range(scratch.shape[0])], axis=1
    )


def spill(scratch, values):
    for lane in range(scratch.shape[0]):
        part = values[:, :, lane * 128 : (lane + 1) * 128].astype(F32)
        scratch[lane] = part.reshape(scratch.shape[1], 128)


def fill(out_ref, scratch):
    for lane in range(scratch.shape[0]):
        part = scratch[lane].reshape(out_ref.shape[0], TILE, 128)
        out_ref[:, :, lane * 128 : (lane + 1) * 128] = part.astype(BF16)


def edges_kernel(pair_ref, mask_ref, gains_ref, w_ref, wg_ref, wb_ref, out_ref, gate_ref, small_ref, scratch):
    rows, total = mask_ref.shape
    width = gains_ref.shape[1]
    small_ref[MASK_AT : MASK_AT + rows, :] = (1000000000.0 * LOG2E) * (mask_ref[...].astype(F32) - 1.0)
    small_ref[GAIN_AT : GAIN_AT + 3, 0:width] = gains_ref[...]
    small_ref[BIAS_AT : BIAS_AT + wb_ref.shape[0], 0:width] = wb_ref[...].astype(F32)
    hidden = out_ref.shape[0]
    normed = [norm_rows(pair_ref[row], gains_ref[0:1, :]) for row in range(rows)]
    edges = [dot(w_ref[...], normed[row], 0, 1) for row in range(rows)]
    for row in range(rows):
        gate_ref[row] = sigmoid(dot(normed[row], wg_ref[...], 1, 0))
    for row in range(rows):
        mask = mask_ref[row : row + 1, :].astype(F32)
        for side in range(2):
            gate = edges[row][2 * side * hidden : (2 * side + 1) * hidden]
            value = edges[row][(2 * side + 1) * hidden : (2 * side + 2) * hidden]
            put_rows(scratch, side * rows + row, TILE, mask * sigmoid(gate) * value)
    fill(out_ref, scratch)


def product_kernel(sides_ref, out_ref, scratch, right_ref, prod_ref):
    devices, _, total = sides_ref.shape
    rows = total // devices
    half = total // 2
    spill(scratch, sides_ref[...])
    for row in range(rows):
        put_rows(right_ref, row, rows, get_rows(scratch, rows + row, devices, TILE))
    right = jnp.concatenate([right_ref[lane] for lane in range(total // 128)], axis=1).astype(BF16)
    left = [get_rows(scratch, row, devices, TILE).astype(BF16) for row in range(rows)]
    product = dot(jnp.concatenate(left, axis=0), right, 1, 1)
    for row in range(rows):
        for part in range(2):
            put_rows(prod_ref, 2 * row + part, TILE, product[row * devices : (row + 1) * devices, part * half : (part + 1) * half])
    fill(out_ref, prod_ref)


def middle_kernel(
    prod_ref,
    pair_ref,
    gate_ref,
    small_ref,
    wo_ref,
    mid_ref,
    normed_ref,
    bias_ref,
    scratch,
    bias_f,
):
    rows, total, width = pair_ref.shape
    heads = 2 * TILE // rows
    devices = bias_ref.shape[0]
    spill(scratch, prod_ref[...])
    gain = small_ref[GAIN_AT + 1 : GAIN_AT + 2, 0:width].T
    wb = small_ref[BIAS_AT : BIAS_AT + heads, 0:width].astype(BF16)
    prod_normed = []
    for row in range(rows):
        prod = jnp.concatenate(
            [get_rows(scratch, 2 * row + part, width, TILE) for part in range(2)], axis=1
        )
        mean = jnp.mean(prod, axis=0, keepdims=True)
        centered = prod - mean
        var = jnp.mean(centered * centered, axis=0, keepdims=True)
        prod_normed.append((centered * lax.rsqrt(var + 1e-05) * gain).astype(BF16))
    update = [dot(prod_normed[row], wo_ref[...], 0, 0) for row in range(rows)]
    mid = [(pair_ref[row].astype(F32) + gate_ref[row] * update[row]).astype(BF16) for row in range(rows)]
    mid_normed = []
    for row in range(rows):
        mid_ref[row] = mid[row]
        mid_normed.append(norm_rows(mid[row], small_ref[GAIN_AT + 2 : GAIN_AT + 3, 0:width]))
        normed_ref[row] = mid_normed[row]
    bias = [dot(wb, mid_normed[row], 1, 1) for row in range(rows)]
    for row in range(rows):
        for head in range(heads):
            bias_f[head * rows + row : head * rows + row + 1, :] = bias[row][head : head + 1, :]
    for part in range(2):
        block = bias_f[part * TILE : (part + 1) * TILE, :].astype(BF16)
        for pair_of in range(devices // 2):
            bias_ref[2 * pair_of + part] = block


def attend(head_dim, first_head, query_ref, key_ref, value_ref, gate_ref, bias_ref, small_ref, scratch, bias_f):
    rows, total, width = value_ref.shape
    devices = bias_ref.shape[0]
    own = TILE // rows
    spill(scratch, bias_ref[...])
    for head in range(own):
        for row in range(rows):
            values = get_rows(scratch, head * rows + row, devices, TILE) * LOG2E
            put_rows(bias_f.at[head], row, rows, values)
    base = first_head[0]
    lane_head = lax.broadcasted_iota(jnp.int32, (1, width), 1) // head_dim
    mine = (lane_head >= base) & (lane_head < base + own)
    attended = []
    for row in range(rows):
        expos, boths = [], []
        for head in range(own):
            pick = (lane_head == base + head).astype(BF16)
            bias = jnp.concatenate([bias_f[head, lane] for lane in range(total // 128)], axis=1)
            logits = dot(query_ref[row] * pick, key_ref[row], 1, 1) + bias + small_ref[MASK_AT + row : MASK_AT + row + 1, :]
            top = jnp.max(logits, axis=-1, keepdims=True)
            expos.append(jnp.exp2(logits - top).astype(BF16))
            value = value_ref[row]
            boths.append(
                jnp.concatenate([value * pick, jnp.broadcast_to(pick, value.shape)], axis=1)
            )
        mixed = dot(jnp.concatenate(expos, axis=1), jnp.concatenate(boths, axis=0), 1, 0)
        share = jnp.where(mine, mixed[:, :width] / mixed[:, width:], 0.0)
        attended.append((gate_ref[row] * share).astype(BF16))
    return attended


def own_heads_kernel(
    head_dim,
    first_head,
    normed_ref,
    bias_ref,
    small_ref,
    win_ref,
    query_ref,
    key_ref,
    value_ref,
    gate_ref,
    out_ref,
    scratch,
    bias_f,
):
    rows, total, width = normed_ref.shape
    scale = LOG2E / math.sqrt(head_dim)
    packed = [dot(normed_ref[row], win_ref[...], 1, 0) for row in range(rows)]
    for row in range(rows):
        query_ref[row] = (packed[row][:, 0:width] * scale).astype(BF16)
        key_ref[row] = packed[row][:, width : 2 * width].astype(BF16)
        value_ref[row] = packed[row][:, 2 * width : 3 * width].astype(BF16)
        gate_ref[row] = sigmoid(packed[row][:, 3 * width : 4 * width])
    attended = attend(
        head_dim, first_head, query_ref, key_ref, value_ref, gate_ref, bias_ref, small_ref, scratch, bias_f
    )
    for row in range(rows):
        out_ref[row] = attended[row]


def other_heads_kernel(
    head_dim,
    first_head,
    query_ref,
    key_ref,
    value_ref,
    gate_ref,
    bias_ref,
    small_ref,
    mid_ref,
    part_ref,
    wout_ref,
    out_ref,
    scratch,
    bias_f,
    result,
    sems,
):
    rows = mid_ref.shape[0]
    attended = attend(
        head_dim, first_head, query_ref, key_ref, value_ref, gate_ref, bias_ref, small_ref, scratch, bias_f
    )
    copies = []
    for row in range(rows):
        update = dot(attended[row] + part_ref[row], wout_ref[...], 1, 0)
        result[row] = (mid_ref[row].astype(F32) + update).astype(BF16)
        copies.append(pltpu.make_async_copy(result.at[row], out_ref.at[row], sems.at[row]))
        copies[row].start()
    for copy in copies:
        copy.wait()


def call(kernel, out_shape, scratch, n_args, scalars=0, limit=VMEM_LIMIT, out_space=pltpu.VMEM):
    specs = [
        pl.BlockSpec(memory_space=pltpu.SMEM if at < scalars else pltpu.VMEM) for at in range(n_args)
    ]
    return pl.pallas_call(
        kernel,
        in_specs=specs,
        out_specs=jax.tree.map(lambda _: pl.BlockSpec(memory_space=out_space), out_shape),
        out_shape=out_shape,
        scratch_shapes=scratch,
        compiler_params=pltpu.CompilerParams(vmem_limit_bytes=limit),
    )


def exchange(array):
    return lax.all_to_all(array, "dap", 0, 0, tiled=True)


def per_device(
    pair, pair_mask, norm_gains, w_edges, w_tri_gate, w_tri_out, w_attn_in, w_tri_bias, w_attn_out
):
    rows, total, width = pair.shape
    hidden = w_tri_out.shape[0]
    heads = w_tri_bias.shape[1]
    head_dim = width // heads
    own = heads // 2
    devices = total // rows
    lanes = total // 128
    shape = jax.ShapeDtypeStruct
    tall = pltpu.VMEM((lanes, devices * TILE, 128), F32)
    square = pltpu.VMEM((lanes, total, 128), F32)
    short = pltpu.VMEM((lanes // 2, devices * TILE, 128), F32)
    sides, gate, small = call(
        edges_kernel,
        [
            shape((hidden, TILE, total), BF16),
            shape((rows, total, width), F32),
            shape((SMALL, total), F32),
        ],
        [tall],
        6,
        limit=EDGES_LIMIT,
    )(pair, pair_mask, norm_gains, w_edges, w_tri_gate, w_tri_bias.T)
    sides = exchange(sides)
    product = call(
        product_kernel, shape((devices, TILE, total // 2), BF16), [tall, square, short], 1
    )(sides)
    product = exchange(product)
    like = shape((rows, total, width), BF16)
    wide = shape((rows, total, width), F32)
    mid, mid_normed, bias = call(
        middle_kernel,
        [like, like, shape((devices, TILE, total), BF16)],
        [short, pltpu.VMEM((2 * TILE, total), F32)],
        5,
    )(product, pair, gate, small, w_tri_out)
    mine = exchange(bias)
    swap = [(d, d ^ 1) for d in range(devices)]
    other = lax.ppermute(mine, "dap", swap)
    core = lax.rem(lax.axis_index("dap"), 2)
    mine_first = jnp.reshape(core * own, (1,))
    other_first = jnp.reshape((1 - core) * own, (1,))
    scratch = [tall, pltpu.VMEM((own, lanes, total, 128), F32)]
    query, key, value, att_gate, part = call(
        functools.partial(own_heads_kernel, head_dim),
        [like, like, like, wide, like],
        scratch,
        5,
        1,
    )(mine_first, mid_normed, mine, small, w_attn_in)
    scratch = scratch + [pltpu.VMEM((rows, total, width), BF16), pltpu.SemaphoreType.DMA((rows,))]
    return call(
        functools.partial(other_heads_kernel, head_dim),
        like,
        scratch,
        10,
        1,
        out_space=pl.ANY,
    )(other_first, query, key, value, att_gate, other, small, mid, part, w_attn_out)


def solution(mesh):
    placed = (P("dap", None, None), P("dap", None), P(), P(), P(), P(), P(), P(), P())
    return jax.shard_map(
        per_device, mesh=mesh, in_specs=placed, out_specs=P("dap", None, None), check_vma=False
    )
```

```python
import functools
import math

import jax
import jax.numpy as jnp
from jax import lax
from jax.experimental import pallas as pl
from jax.experimental.pallas import tpu as pltpu
from jax.sharding import PartitionSpec as P

F32 = jnp.float32
BF16 = jnp.bfloat16
VMEM_LIMIT = 40 * 1024 * 1024
EDGES_LIMIT = 60 * 1024 * 1024
LOG2E = math.log2(math.e)
TILE = 8
MASK_AT, GAIN_AT, BIAS_AT, SMALL = 0, 8, 16, 24


def dot(a, b, ca, cb):
    return lax.dot_general(a, b, (((ca,), (cb,)), ((), ())), preferred_element_type=F32)


def sigmoid(x):
    return 0.5 + 0.5 * jnp.tanh(0.5 * x)


def norm_rows(values, gain):
    size = values.shape[-1]
    row = lax.broadcasted_iota(jnp.int32, (size, size), 0)
    col = lax.broadcasted_iota(jnp.int32, (size, size), 1)
    centering = ((row == col).astype(F32) - 1.0 / size).astype(BF16)
    average = jnp.full((size, size), 1.0 / size, BF16)
    centered = dot(values, centering, 1, 0)
    var = dot((centered * centered).astype(BF16), average, 1, 0)
    return (centered * lax.rsqrt(var + 1e-05) * gain).astype(BF16)


def put_rows(scratch, start, stride, values):
    for lane in range(values.shape[1] // 128):
        scratch[lane, pl.ds(start, values.shape[0], stride=stride), :] = values[:, lane * 128 : (lane + 1) * 128]


def get_rows(scratch, start, size, stride):
    return jnp.concatenate(
        [scratch[lane, pl.ds(start, size, stride=stride), :] for lane in range(scratch.shape[0])], axis=1
    )


def spill(scratch, values):
    for lane in range(scratch.shape[0]):
        part = values[:, :, lane * 128 : (lane + 1) * 128].astype(F32)
        scratch[lane] = part.reshape(scratch.shape[1], 128)


def fill(out_ref, scratch):
    for lane in range(scratch.shape[0]):
        part = scratch[lane].reshape(out_ref.shape[0], TILE, 128)
        out_ref[:, :, lane * 128 : (lane + 1) * 128] = part.astype(BF16)


def edges_kernel(pair_ref, mask_ref, gains_ref, w_ref, out_ref, scratch):
    rows, total = mask_ref.shape
    hidden = out_ref.shape[0]
    normed = [norm_rows(pair_ref[row], gains_ref[0:1, :]) for row in range(rows)]
    edges = [dot(w_ref[...], normed[row], 0, 1) for row in range(rows)]
    for row in range(rows):
        mask = mask_ref[row : row + 1, :].astype(F32)
        for side in range(2):
            gate = edges[row][2 * side * hidden : (2 * side + 1) * hidden]
            value = edges[row][(2 * side + 1) * hidden : (2 * side + 2) * hidden]
            put_rows(scratch, side * rows + row, TILE, mask * sigmoid(gate) * value)
    fill(out_ref, scratch)


def gate_kernel(pair_ref, mask_ref, gains_ref, wg_ref, wb_ref, gate_ref, small_ref):
    rows = mask_ref.shape[0]
    width = gains_ref.shape[1]
    small_ref[MASK_AT : MASK_AT + rows, :] = (1000000000.0 * LOG2E) * (mask_ref[...].astype(F32) - 1.0)
    small_ref[GAIN_AT : GAIN_AT + 3, 0:width] = gains_ref[...]
    small_ref[BIAS_AT : BIAS_AT + wb_ref.shape[0], 0:width] = wb_ref[...].astype(F32)
    normed = [norm_rows(pair_ref[row], gains_ref[0:1, :]) for row in range(rows)]
    for row in range(rows):
        gate_ref[row] = sigmoid(dot(normed[row], wg_ref[...], 1, 0))


def product_kernel(sides_ref, out_ref, scratch, right_ref, prod_ref):
    devices, _, total = sides_ref.shape
    rows = total // devices
    half = total // 2
    spill(scratch, sides_ref[...])
    for row in range(rows):
        put_rows(right_ref, row, rows, get_rows(scratch, rows + row, devices, TILE))
    right = jnp.concatenate([right_ref[lane] for lane in range(total // 128)], axis=1).astype(BF16)
    left = [get_rows(scratch, row, devices, TILE).astype(BF16) for row in range(rows)]
    product = dot(jnp.concatenate(left, axis=0), right, 1, 1)
    for row in range(rows):
        for part in range(2):
            put_rows(prod_ref, 2 * row + part, TILE, product[row * devices : (row + 1) * devices, part * half : (part + 1) * half])
    fill(out_ref, prod_ref)


def middle_kernel(
    prod_ref,
    pair_ref,
    gate_ref,
    small_ref,
    wo_ref,
    mid_ref,
    normed_ref,
    bias_ref,
    scratch,
    bias_f,
):
    rows, total, width = pair_ref.shape
    heads = 2 * TILE // rows
    devices = bias_ref.shape[0]
    spill(scratch, prod_ref[...])
    gain = small_ref[GAIN_AT + 1 : GAIN_AT + 2, 0:width].T
    wb = small_ref[BIAS_AT : BIAS_AT + heads, 0:width].astype(BF16)
    prod_normed = []
    for row in range(rows):
        prod = jnp.concatenate(
            [get_rows(scratch, 2 * row + part, width, TILE) for part in range(2)], axis=1
        )
        mean = jnp.mean(prod, axis=0, keepdims=True)
        centered = prod - mean
        var = jnp.mean(centered * centered, axis=0, keepdims=True)
        prod_normed.append((centered * lax.rsqrt(var + 1e-05) * gain).astype(BF16))
    update = [dot(prod_normed[row], wo_ref[...], 0, 0) for row in range(rows)]
    mid = [(pair_ref[row].astype(F32) + gate_ref[row] * update[row]).astype(BF16) for row in range(rows)]
    mid_normed = []
    for row in range(rows):
        mid_ref[row] = mid[row]
        mid_normed.append(norm_rows(mid[row], small_ref[GAIN_AT + 2 : GAIN_AT + 3, 0:width]))
        normed_ref[row] = mid_normed[row]
    bias = [dot(wb, mid_normed[row], 1, 1) for row in range(rows)]
    for row in range(rows):
        for head in range(heads):
            bias_f[head * rows + row : head * rows + row + 1, :] = bias[row][head : head + 1, :]
    for part in range(2):
        block = bias_f[part * TILE : (part + 1) * TILE, :].astype(BF16)
        for pair_of in range(devices // 2):
            bias_ref[2 * pair_of + part] = block


def attend(head_dim, first_head, query_ref, key_ref, value_ref, gate_ref, bias_ref, small_ref, scratch, bias_f):
    rows, total, width = value_ref.shape
    devices = bias_ref.shape[0]
    own = TILE // rows
    spill(scratch, bias_ref[...])
    for head in range(own):
        for row in range(rows):
            values = get_rows(scratch, head * rows + row, devices, TILE) * LOG2E
            put_rows(bias_f.at[head], row, rows, values)
    base = first_head[0]
    lane_head = lax.broadcasted_iota(jnp.int32, (1, width), 1) // head_dim
    mine = (lane_head >= base) & (lane_head < base + own)
    attended = []
    for row in range(rows):
        expos, boths = [], []
        for head in range(own):
            pick = (lane_head == base + head).astype(BF16)
            bias = jnp.concatenate([bias_f[head, lane] for lane in range(total // 128)], axis=1)
            logits = dot(query_ref[row] * pick, key_ref[row], 1, 1) + bias + small_ref[MASK_AT + row : MASK_AT + row + 1, :]
            top = jnp.max(logits, axis=-1, keepdims=True)
            expos.append(jnp.exp2(logits - top).astype(BF16))
            value = value_ref[row]
            boths.append(
                jnp.concatenate([value * pick, jnp.broadcast_to(pick, value.shape)], axis=1)
            )
        mixed = dot(jnp.concatenate(expos, axis=1), jnp.concatenate(boths, axis=0), 1, 0)
        share = jnp.where(mine, mixed[:, :width] / mixed[:, width:], 0.0)
        attended.append((gate_ref[row] * share).astype(BF16))
    return attended


def own_heads_kernel(
    head_dim,
    first_head,
    normed_ref,
    bias_ref,
    small_ref,
    win_ref,
    query_ref,
    key_ref,
    value_ref,
    gate_ref,
    out_ref,
    scratch,
    bias_f,
):
    rows, total, width = normed_ref.shape
    scale = LOG2E / math.sqrt(head_dim)
    packed = [dot(normed_ref[row], win_ref[...], 1, 0) for row in range(rows)]
    for row in range(rows):
        query_ref[row] = (packed[row][:, 0:width] * scale).astype(BF16)
        key_ref[row] = packed[row][:, width : 2 * width].astype(BF16)
        value_ref[row] = packed[row][:, 2 * width : 3 * width].astype(BF16)
        gate_ref[row] = sigmoid(packed[row][:, 3 * width : 4 * width])
    attended = attend(
        head_dim, first_head, query_ref, key_ref, value_ref, gate_ref, bias_ref, small_ref, scratch, bias_f
    )
    for row in range(rows):
        out_ref[row] = attended[row]


def other_heads_kernel(
    head_dim,
    first_head,
    query_ref,
    key_ref,
    value_ref,
    gate_ref,
    bias_ref,
    small_ref,
    mid_ref,
    part_ref,
    wout_ref,
    out_ref,
    scratch,
    bias_f,
    result,
    sems,
):
    rows = mid_ref.shape[0]
    attended = attend(
        head_dim, first_head, query_ref, key_ref, value_ref, gate_ref, bias_ref, small_ref, scratch, bias_f
    )
    copies = []
    for row in range(rows):
        update = dot(attended[row] + part_ref[row], wout_ref[...], 1, 0)
        result[row] = (mid_ref[row].astype(F32) + update).astype(BF16)
        copies.append(pltpu.make_async_copy(result.at[row], out_ref.at[row], sems.at[row]))
        copies[row].start()
    for copy in copies:
        copy.wait()


def call(kernel, out_shape, scratch, n_args, scalars=0, limit=VMEM_LIMIT, out_space=pltpu.VMEM, cost=None):
    specs = [
        pl.BlockSpec(memory_space=pltpu.SMEM if at < scalars else pltpu.VMEM) for at in range(n_args)
    ]
    return pl.pallas_call(
        kernel,
        in_specs=specs,
        out_specs=jax.tree.map(lambda _: pl.BlockSpec(memory_space=out_space), out_shape),
        out_shape=out_shape,
        scratch_shapes=scratch,
        compiler_params=pltpu.CompilerParams(vmem_limit_bytes=limit),
        cost_estimate=cost,
    )


def exchange(array):
    return lax.all_to_all(array, "dap", 0, 0, tiled=True)


def per_device(
    pair, pair_mask, norm_gains, w_edges, w_tri_gate, w_tri_out, w_attn_in, w_tri_bias, w_attn_out
):
    rows, total, width = pair.shape
    hidden = w_tri_out.shape[0]
    heads = w_tri_bias.shape[1]
    head_dim = width // heads
    own = heads // 2
    devices = total // rows
    lanes = total // 128
    shape = jax.ShapeDtypeStruct
    tall = pltpu.VMEM((lanes, devices * TILE, 128), F32)
    square = pltpu.VMEM((lanes, total, 128), F32)
    short = pltpu.VMEM((lanes // 2, devices * TILE, 128), F32)
    sides = call(
        edges_kernel, shape((hidden, TILE, total), BF16), [tall], 4, limit=EDGES_LIMIT
    )(pair, pair_mask, norm_gains, w_edges)
    gate, small = call(
        gate_kernel,
        [shape((rows, total, width), F32), shape((SMALL, total), F32)],
        [],
        5,
        cost=pl.CostEstimate(
            flops=2 * rows * total * width * width,
            bytes_accessed=4 * rows * total * width,
            transcendentals=rows * total * width,
        ),
    )(pair, pair_mask, norm_gains, w_tri_gate, w_tri_bias.T)
    sides = exchange(sides)
    sides, gate, small = lax.optimization_barrier((sides, gate, small))
    product = call(
        product_kernel, shape((devices, TILE, total // 2), BF16), [tall, square, short], 1
    )(sides)
    product = exchange(product)
    like = shape((rows, total, width), BF16)
    wide = shape((rows, total, width), F32)
    mid, mid_normed, bias = call(
        middle_kernel,
        [like, like, shape((devices, TILE, total), BF16)],
        [short, pltpu.VMEM((2 * TILE, total), F32)],
        5,
    )(product, pair, gate, small, w_tri_out)
    mine = exchange(bias)
    swap = [(d, d ^ 1) for d in range(devices)]
    other = lax.ppermute(mine, "dap", swap)
    core = lax.rem(lax.axis_index("dap"), 2)
    mine_first = jnp.reshape(core * own, (1,))
    other_first = jnp.reshape((1 - core) * own, (1,))
    scratch = [tall, pltpu.VMEM((own, lanes, total, 128), F32)]
    query, key, value, att_gate, part = call(
        functools.partial(own_heads_kernel, head_dim),
        [like, like, like, wide, like],
        scratch,
        5,
        1,
    )(mine_first, mid_normed, mine, small, w_attn_in)
    scratch = scratch + [pltpu.VMEM((rows, total, width), BF16), pltpu.SemaphoreType.DMA((rows,))]
    return call(
        functools.partial(other_heads_kernel, head_dim),
        like,
        scratch,
        10,
        1,
        out_space=pl.ANY,
    )(other_first, query, key, value, att_gate, other, small, mid, part, w_attn_out)


def solution(mesh):
    placed = (P("dap", None, None), P("dap", None), P(), P(), P(), P(), P(), P(), P())
    return jax.shard_map(
        per_device, mesh=mesh, in_specs=placed, out_specs=P("dap", None, None), check_vma=False
    )
```

```python
import functools
import math

import jax
import jax.numpy as jnp
from jax import lax
from jax.experimental import pallas as pl
from jax.experimental.pallas import tpu as pltpu
from jax.sharding import PartitionSpec as P

F32 = jnp.float32
BF16 = jnp.bfloat16
VMEM_LIMIT = 40 * 1024 * 1024
EDGES_LIMIT = 60 * 1024 * 1024
LOG2E = math.log2(math.e)
TILE = 8
MASK_AT, GAIN_AT, BIAS_AT, SMALL = 0, 8, 16, 24


def dot(a, b, ca, cb):
    return lax.dot_general(a, b, (((ca,), (cb,)), ((), ())), preferred_element_type=F32)


def sigmoid(x):
    return 0.5 + 0.5 * jnp.tanh(0.5 * x)


def norm_rows(values, gain):
    size = values.shape[-1]
    row = lax.broadcasted_iota(jnp.int32, (size, size), 0)
    col = lax.broadcasted_iota(jnp.int32, (size, size), 1)
    centering = ((row == col).astype(F32) - 1.0 / size).astype(BF16)
    average = jnp.full((size, size), 1.0 / size, BF16)
    centered = dot(values, centering, 1, 0)
    var = dot((centered * centered).astype(BF16), average, 1, 0)
    return (centered * lax.rsqrt(var + 1e-05) * gain).astype(BF16)


def put_rows(scratch, start, stride, values):
    for lane in range(values.shape[1] // 128):
        scratch[lane, pl.ds(start, values.shape[0], stride=stride), :] = values[:, lane * 128 : (lane + 1) * 128]


def get_rows(scratch, start, size, stride):
    return jnp.concatenate(
        [scratch[lane, pl.ds(start, size, stride=stride), :] for lane in range(scratch.shape[0])], axis=1
    )


def spill(scratch, values):
    for lane in range(scratch.shape[0]):
        part = values[:, :, lane * 128 : (lane + 1) * 128].astype(F32)
        scratch[lane] = part.reshape(scratch.shape[1], 128)


def fill(out_ref, scratch):
    for lane in range(scratch.shape[0]):
        part = scratch[lane].reshape(out_ref.shape[0], TILE, 128)
        out_ref[:, :, lane * 128 : (lane + 1) * 128] = part.astype(BF16)


def edges_kernel(
    pair_any, mask_any, gains_any, w_any, out_any, scratch, pair_ref, mask_ref, gains_ref, w_ref, out_ref, sems
):
    rows, total = mask_ref.shape
    hidden = out_ref.shape[0]
    arrays = ((pair_any, pair_ref), (mask_any, mask_ref), (gains_any, gains_ref), (w_any, w_ref))
    copies = [pltpu.make_async_copy(src, dst, sems.at[at]) for at, (src, dst) in enumerate(arrays)]
    for copy in copies:
        copy.start()
    for copy in copies:
        copy.wait()
    normed = [norm_rows(pair_ref[row], gains_ref[0:1, :]) for row in range(rows)]
    edges = [dot(normed[row], w_ref[...], 1, 0) for row in range(rows)]
    for row in range(rows):
        mask = mask_ref[row : row + 1, :].astype(F32)
        for side in range(2):
            gate = edges[row][:, 2 * side * hidden : (2 * side + 1) * hidden]
            value = edges[row][:, (2 * side + 1) * hidden : (2 * side + 2) * hidden]
            put_rows(scratch, side * rows + row, TILE, mask * (sigmoid(gate) * value).T)
    copies = []
    for lane in range(scratch.shape[0]):
        here = slice(lane * 128, (lane + 1) * 128)
        out_ref[:, :, here] = scratch[lane].reshape(hidden, TILE, 128).astype(BF16)
        copies.append(pltpu.make_async_copy(out_ref.at[:, :, here], out_any.at[:, :, here], sems.at[4 + lane]))
        copies[lane].start()
    for copy in copies:
        copy.wait()


def gate_kernel(pair_ref, mask_ref, gains_ref, wg_ref, wb_ref, gate_ref, small_ref):
    rows = mask_ref.shape[0]
    width = gains_ref.shape[1]
    small_ref[MASK_AT : MASK_AT + rows, :] = (1000000000.0 * LOG2E) * (mask_ref[...].astype(F32) - 1.0)
    small_ref[GAIN_AT : GAIN_AT + 3, 0:width] = gains_ref[...]
    small_ref[BIAS_AT : BIAS_AT + wb_ref.shape[0], 0:width] = wb_ref[...].astype(F32)
    normed = [norm_rows(pair_ref[row], gains_ref[0:1, :]) for row in range(rows)]
    for row in range(rows):
        gate_ref[row] = sigmoid(dot(normed[row], wg_ref[...], 1, 0))


def product_kernel(sides_ref, out_ref, scratch, right_ref, prod_ref):
    devices, _, total = sides_ref.shape
    rows = total // devices
    half = total // 2
    spill(scratch, sides_ref[...])
    for row in range(rows):
        put_rows(right_ref, row, rows, get_rows(scratch, rows + row, devices, TILE))
    right = jnp.concatenate([right_ref[lane] for lane in range(total // 128)], axis=1).astype(BF16)
    left = [get_rows(scratch, row, devices, TILE).astype(BF16) for row in range(rows)]
    product = dot(jnp.concatenate(left, axis=0), right, 1, 1)
    for row in range(rows):
        for part in range(2):
            put_rows(prod_ref, 2 * row + part, TILE, product[row * devices : (row + 1) * devices, part * half : (part + 1) * half])
    fill(out_ref, prod_ref)


def middle_kernel(
    prod_ref,
    pair_ref,
    gate_ref,
    small_ref,
    wo_ref,
    mid_ref,
    normed_ref,
    bias_ref,
    scratch,
    bias_f,
):
    rows, total, width = pair_ref.shape
    heads = 2 * TILE // rows
    devices = bias_ref.shape[0]
    spill(scratch, prod_ref[...])
    gain = small_ref[GAIN_AT + 1 : GAIN_AT + 2, 0:width].T
    wb = small_ref[BIAS_AT : BIAS_AT + heads, 0:width].astype(BF16)
    prod_normed = []
    for row in range(rows):
        prod = jnp.concatenate(
            [get_rows(scratch, 2 * row + part, width, TILE) for part in range(2)], axis=1
        )
        mean = jnp.mean(prod, axis=0, keepdims=True)
        centered = prod - mean
        var = jnp.mean(centered * centered, axis=0, keepdims=True)
        prod_normed.append((centered * lax.rsqrt(var + 1e-05) * gain).astype(BF16))
    update = [dot(prod_normed[row], wo_ref[...], 0, 0) for row in range(rows)]
    mid = [(pair_ref[row].astype(F32) + gate_ref[row] * update[row]).astype(BF16) for row in range(rows)]
    mid_normed = []
    for row in range(rows):
        mid_ref[row] = mid[row]
        mid_normed.append(norm_rows(mid[row], small_ref[GAIN_AT + 2 : GAIN_AT + 3, 0:width]))
        normed_ref[row] = mid_normed[row]
    bias = [dot(wb, mid_normed[row], 1, 1) for row in range(rows)]
    for row in range(rows):
        for head in range(heads):
            bias_f[head * rows + row : head * rows + row + 1, :] = bias[row][head : head + 1, :]
    for part in range(2):
        block = bias_f[part * TILE : (part + 1) * TILE, :].astype(BF16)
        for pair_of in range(devices // 2):
            bias_ref[2 * pair_of + part] = block


def attend(head_dim, first_head, query_ref, key_ref, value_ref, gate_ref, bias_ref, small_ref, scratch, bias_f):
    rows, total, width = value_ref.shape
    devices = bias_ref.shape[0]
    own = TILE // rows
    spill(scratch, bias_ref[...])
    for head in range(own):
        for row in range(rows):
            values = get_rows(scratch, head * rows + row, devices, TILE) * LOG2E
            put_rows(bias_f.at[head], row, rows, values)
    base = first_head[0]
    lane_head = lax.broadcasted_iota(jnp.int32, (1, width), 1) // head_dim
    mine = (lane_head >= base) & (lane_head < base + own)
    step = total // 4
    picks = [(lane_head == base + head).astype(BF16) for head in range(own)]
    attended = []
    for row in range(rows):
        value = value_ref[row]
        both = jnp.concatenate(
            [jnp.concatenate([value * pick, jnp.broadcast_to(pick, value.shape)], axis=1) for pick in picks],
            axis=0,
        )
        mixed = []
        for at in range(0, total, step):
            here = slice(at, at + step)
            expos = []
            for head in range(own):
                bias = jnp.concatenate([bias_f[head, lane, here] for lane in range(total // 128)], axis=1)
                logits = dot(query_ref[row, here] * picks[head], key_ref[row], 1, 1) + bias
                logits = logits + small_ref[MASK_AT + row : MASK_AT + row + 1, :]
                top = jnp.max(logits, axis=-1, keepdims=True)
                expos.append(jnp.exp2(logits - top).astype(BF16))
            mixed.append(dot(jnp.concatenate(expos, axis=1), both, 1, 0))
        mixed = jnp.concatenate(mixed, axis=0)
        share = jnp.where(mine, mixed[:, :width] / mixed[:, width:], 0.0)
        attended.append((gate_ref[row] * share).astype(BF16))
    return attended


def own_heads_kernel(
    head_dim,
    first_head,
    normed_ref,
    bias_ref,
    small_ref,
    win_ref,
    query_ref,
    key_ref,
    value_ref,
    gate_ref,
    out_ref,
    scratch,
    bias_f,
):
    rows, total, width = normed_ref.shape
    scale = LOG2E / math.sqrt(head_dim)
    packed = [dot(normed_ref[row], win_ref[...], 1, 0) for row in range(rows)]
    for row in range(rows):
        query_ref[row] = (packed[row][:, 0:width] * scale).astype(BF16)
        key_ref[row] = packed[row][:, width : 2 * width].astype(BF16)
        value_ref[row] = packed[row][:, 2 * width : 3 * width].astype(BF16)
        gate_ref[row] = sigmoid(packed[row][:, 3 * width : 4 * width])
    attended = attend(
        head_dim, first_head, query_ref, key_ref, value_ref, gate_ref, bias_ref, small_ref, scratch, bias_f
    )
    for row in range(rows):
        out_ref[row] = attended[row]


def other_heads_kernel(
    head_dim,
    first_head,
    query_ref,
    key_ref,
    value_ref,
    gate_ref,
    bias_ref,
    small_ref,
    mid_ref,
    part_ref,
    wout_ref,
    out_ref,
    scratch,
    bias_f,
    result,
    sems,
):
    rows = mid_ref.shape[0]
    attended = attend(
        head_dim, first_head, query_ref, key_ref, value_ref, gate_ref, bias_ref, small_ref, scratch, bias_f
    )
    copies = []
    for row in range(rows):
        update = dot(attended[row] + part_ref[row], wout_ref[...], 1, 0)
        result[row] = (mid_ref[row].astype(F32) + update).astype(BF16)
        copies.append(pltpu.make_async_copy(result.at[row], out_ref.at[row], sems.at[row]))
        copies[row].start()
    for copy in copies:
        copy.wait()


def call(kernel, out_shape, scratch, n_args, scalars=0, limit=VMEM_LIMIT, in_space=pltpu.VMEM, out_space=pltpu.VMEM, cost=None):
    specs = [
        pl.BlockSpec(memory_space=pltpu.SMEM if at < scalars else in_space) for at in range(n_args)
    ]
    return pl.pallas_call(
        kernel,
        in_specs=specs,
        out_specs=jax.tree.map(lambda _: pl.BlockSpec(memory_space=out_space), out_shape),
        out_shape=out_shape,
        scratch_shapes=scratch,
        compiler_params=pltpu.CompilerParams(vmem_limit_bytes=limit),
        cost_estimate=cost,
    )


def exchange(array):
    return lax.all_to_all(array, "dap", 0, 0, tiled=True)


def per_device(
    pair, pair_mask, norm_gains, w_edges, w_tri_gate, w_tri_out, w_attn_in, w_tri_bias, w_attn_out
):
    rows, total, width = pair.shape
    hidden = w_tri_out.shape[0]
    heads = w_tri_bias.shape[1]
    head_dim = width // heads
    own = heads // 2
    devices = total // rows
    lanes = total // 128
    shape = jax.ShapeDtypeStruct
    tall = pltpu.VMEM((lanes, devices * TILE, 128), F32)
    square = pltpu.VMEM((lanes, total, 128), F32)
    short = pltpu.VMEM((lanes // 2, devices * TILE, 128), F32)
    inputs = [pair, pair_mask, norm_gains, w_edges]
    kept = [pltpu.VMEM(array.shape, array.dtype) for array in inputs]
    sides = call(
        edges_kernel,
        shape((hidden, TILE, total), BF16),
        [tall] + kept + [pltpu.VMEM((hidden, TILE, total), BF16), pltpu.SemaphoreType.DMA((4 + lanes,))],
        4,
        limit=EDGES_LIMIT,
        in_space=pl.ANY,
        out_space=pl.ANY,
    )(*inputs)
    gate, small = call(
        gate_kernel,
        [shape((rows, total, width), F32), shape((SMALL, total), F32)],
        [],
        5,
        cost=pl.CostEstimate(
            flops=2 * rows * total * width * width,
            bytes_accessed=4 * rows * total * width,
            transcendentals=rows * total * width,
        ),
    )(pair, pair_mask, norm_gains, w_tri_gate, w_tri_bias.T)
    sides = exchange(sides)
    sides, gate, small = lax.optimization_barrier((sides, gate, small))
    product = call(
        product_kernel, shape((devices, TILE, total // 2), BF16), [tall, square, short], 1
    )(sides)
    product = exchange(product)
    like = shape((rows, total, width), BF16)
    wide = shape((rows, total, width), F32)
    mid, mid_normed, bias = call(
        middle_kernel,
        [like, like, shape((devices, TILE, total), BF16)],
        [short, pltpu.VMEM((2 * TILE, total), F32)],
        5,
    )(product, pair, gate, small, w_tri_out)
    mine = exchange(bias)
    swap = [(d, d ^ 1) for d in range(devices)]
    other = lax.ppermute(mine, "dap", swap)
    core = lax.rem(lax.axis_index("dap"), 2)
    mine_first = jnp.reshape(core * own, (1,))
    other_first = jnp.reshape((1 - core) * own, (1,))
    scratch = [tall, pltpu.VMEM((own, lanes, total, 128), F32)]
    query, key, value, att_gate, part = call(
        functools.partial(own_heads_kernel, head_dim),
        [like, like, like, wide, like],
        scratch,
        5,
        1,
    )(mine_first, mid_normed, mine, small, w_attn_in)
    scratch = scratch + [pltpu.VMEM((rows, total, width), BF16), pltpu.SemaphoreType.DMA((rows,))]
    return call(
        functools.partial(other_heads_kernel, head_dim),
        like,
        scratch,
        10,
        1,
        out_space=pl.ANY,
    )(other_first, query, key, value, att_gate, other, small, mid, part, w_attn_out)


def solution(mesh):
    placed = (P("dap", None, None), P("dap", None), P(), P(), P(), P(), P(), P(), P())
    return jax.shard_map(
        per_device, mesh=mesh, in_specs=placed, out_specs=P("dap", None, None), check_vma=False
    )
```

```python
import functools
import math

import jax
import jax.numpy as jnp
from jax import lax
from jax.experimental import pallas as pl
from jax.experimental.pallas import tpu as pltpu
from jax.sharding import PartitionSpec as P

F32 = jnp.float32
BF16 = jnp.bfloat16
VMEM_LIMIT = 40 * 1024 * 1024
EDGES_LIMIT = 60 * 1024 * 1024
LOG2E = math.log2(math.e)
TILE = 8
MASK_AT, GAIN_AT, BIAS_AT, SMALL = 0, 8, 16, 24


def dot(a, b, ca, cb):
    return lax.dot_general(a, b, (((ca,), (cb,)), ((), ())), preferred_element_type=F32)


def sigmoid(x):
    return 0.5 + 0.5 * jnp.tanh(0.5 * x)


def norm_rows(values, gain):
    size = values.shape[-1]
    row = lax.broadcasted_iota(jnp.int32, (size, size), 0)
    col = lax.broadcasted_iota(jnp.int32, (size, size), 1)
    centering = ((row == col).astype(F32) - 1.0 / size).astype(BF16)
    average = jnp.full((size, size), 1.0 / size, BF16)
    centered = dot(values, centering, 1, 0)
    var = dot((centered * centered).astype(BF16), average, 1, 0)
    return (centered * lax.rsqrt(var + 1e-05) * gain).astype(BF16)


def put_rows(scratch, start, stride, values):
    for lane in range(values.shape[1] // 128):
        scratch[lane, pl.ds(start, values.shape[0], stride=stride), :] = values[:, lane * 128 : (lane + 1) * 128]


def get_rows(scratch, start, size, stride):
    return jnp.concatenate(
        [scratch[lane, pl.ds(start, size, stride=stride), :] for lane in range(scratch.shape[0])], axis=1
    )


def spill(scratch, values):
    for lane in range(scratch.shape[0]):
        part = values[:, :, lane * 128 : (lane + 1) * 128].astype(F32)
        scratch[lane, 0 : values.shape[0] * TILE, :] = part.reshape(values.shape[0] * TILE, 128)


def fill(out_ref, scratch):
    for lane in range(scratch.shape[0]):
        part = scratch[lane, 0 : out_ref.shape[0] * TILE, :].reshape(out_ref.shape[0], TILE, 128)
        out_ref[:, :, lane * 128 : (lane + 1) * 128] = part.astype(BF16)


def edges_kernel(
    pair_any, mask_any, gains_any, w_any, out_any, scratch, pair_ref, mask_ref, gains_ref, w_ref, out_ref, sems
):
    rows, total = mask_ref.shape
    hidden = out_ref.shape[0]
    arrays = ((pair_any, pair_ref), (mask_any, mask_ref), (gains_any, gains_ref), (w_any, w_ref))
    copies = [pltpu.make_async_copy(src, dst, sems.at[at]) for at, (src, dst) in enumerate(arrays)]
    for copy in copies:
        copy.start()
    for copy in copies:
        copy.wait()
    normed = [norm_rows(pair_ref[row], gains_ref[0:1, :]) for row in range(rows)]
    edges = [dot(normed[row], w_ref[...], 1, 0) for row in range(rows)]
    for row in range(rows):
        mask = mask_ref[row : row + 1, :].astype(F32)
        for side in range(2):
            gate = edges[row][:, 2 * side * hidden : (2 * side + 1) * hidden]
            value = edges[row][:, (2 * side + 1) * hidden : (2 * side + 2) * hidden]
            put_rows(scratch, side * rows + row, TILE, mask * (sigmoid(gate) * value).T)
    copies = []
    for lane in range(scratch.shape[0]):
        here = slice(lane * 128, (lane + 1) * 128)
        out_ref[:, :, here] = scratch[lane, 0 : hidden * TILE, :].reshape(hidden, TILE, 128).astype(BF16)
        copies.append(pltpu.make_async_copy(out_ref.at[:, :, here], out_any.at[:, :, here], sems.at[4 + lane]))
        copies[lane].start()
    for copy in copies:
        copy.wait()


def gate_kernel(pair_ref, mask_ref, gains_ref, wg_ref, wb_ref, gate_ref, small_ref):
    rows = mask_ref.shape[0]
    width = gains_ref.shape[1]
    small_ref[MASK_AT : MASK_AT + rows, :] = (1000000000.0 * LOG2E) * (mask_ref[...].astype(F32) - 1.0)
    small_ref[GAIN_AT : GAIN_AT + 3, 0:width] = gains_ref[...]
    small_ref[BIAS_AT : BIAS_AT + wb_ref.shape[0], 0:width] = wb_ref[...].astype(F32)
    normed = [norm_rows(pair_ref[row], gains_ref[0:1, :]) for row in range(rows)]
    for row in range(rows):
        gate_ref[row] = sigmoid(dot(normed[row], wg_ref[...], 1, 0))


def product_kernel(sides_ref, out_ref, scratch, right_ref, prod_ref):
    devices, _, total = sides_ref.shape
    rows = total // devices
    half = total // 2
    spill(scratch, sides_ref[...])
    for row in range(rows):
        put_rows(right_ref, row, rows, get_rows(scratch, rows + row, devices, TILE))
    right = jnp.concatenate([right_ref[lane, 0:total, :] for lane in range(total // 128)], axis=1).astype(BF16)
    left = [get_rows(scratch, row, devices, TILE).astype(BF16) for row in range(rows)]
    product = dot(jnp.concatenate(left, axis=0), right, 1, 1)
    for row in range(rows):
        for part in range(2):
            put_rows(prod_ref, 2 * row + part, TILE, product[row * devices : (row + 1) * devices, part * half : (part + 1) * half])
    fill(out_ref, prod_ref)


def middle_kernel(
    prod_ref,
    pair_ref,
    gate_ref,
    small_ref,
    wo_ref,
    mid_ref,
    normed_ref,
    bias_ref,
    scratch,
    bias_f,
):
    rows, total, width = pair_ref.shape
    heads = 2 * TILE // rows
    devices = bias_ref.shape[0]
    spill(scratch, prod_ref[...])
    gain = small_ref[GAIN_AT + 1 : GAIN_AT + 2, 0:width].T
    wb = small_ref[BIAS_AT : BIAS_AT + heads, 0:width].astype(BF16)
    prod_normed = []
    for row in range(rows):
        prod = jnp.concatenate(
            [get_rows(scratch, 2 * row + part, width, TILE) for part in range(2)], axis=1
        )
        mean = jnp.mean(prod, axis=0, keepdims=True)
        centered = prod - mean
        var = jnp.mean(centered * centered, axis=0, keepdims=True)
        prod_normed.append((centered * lax.rsqrt(var + 1e-05) * gain).astype(BF16))
    update = [dot(prod_normed[row], wo_ref[...], 0, 0) for row in range(rows)]
    mid = [(pair_ref[row].astype(F32) + gate_ref[row] * update[row]).astype(BF16) for row in range(rows)]
    mid_normed = []
    for row in range(rows):
        mid_ref[row] = mid[row]
        mid_normed.append(norm_rows(mid[row], small_ref[GAIN_AT + 2 : GAIN_AT + 3, 0:width]))
        normed_ref[row] = mid_normed[row]
    bias = [dot(wb, mid_normed[row], 1, 1) for row in range(rows)]
    for row in range(rows):
        for head in range(heads):
            bias_f[head * rows + row : head * rows + row + 1, :] = bias[row][head : head + 1, :]
    for part in range(2):
        block = bias_f[part * TILE : (part + 1) * TILE, :].astype(BF16)
        for pair_of in range(devices // 2):
            bias_ref[2 * pair_of + part] = block


def attend(head_dim, first_head, query_ref, key_ref, value_ref, gate_ref, bias_ref, small_ref, scratch, bias_f):
    rows, total, width = value_ref.shape
    devices = bias_ref.shape[0]
    own = TILE // rows
    spill(scratch, bias_ref[...])
    for head in range(own):
        for row in range(rows):
            values = get_rows(scratch, head * rows + row, devices, TILE) * LOG2E
            put_rows(bias_f.at[head], row, rows, values)
    base = first_head[0]
    lane_head = lax.broadcasted_iota(jnp.int32, (1, width), 1) // head_dim
    mine = (lane_head >= base) & (lane_head < base + own)
    step = total // 4
    picks = [(lane_head == base + head).astype(BF16) for head in range(own)]
    attended = []
    for row in range(rows):
        value = value_ref[row]
        both = jnp.concatenate(
            [jnp.concatenate([value * pick, jnp.broadcast_to(pick, value.shape)], axis=1) for pick in picks],
            axis=0,
        )
        mixed = []
        for at in range(0, total, step):
            here = slice(at, at + step)
            expos = []
            for head in range(own):
                bias = jnp.concatenate([bias_f[head, lane, here] for lane in range(total // 128)], axis=1)
                logits = dot(query_ref[row, here] * picks[head], key_ref[row], 1, 1) + bias
                logits = logits + small_ref[MASK_AT + row : MASK_AT + row + 1, :]
                top = jnp.max(logits, axis=-1, keepdims=True)
                expos.append(jnp.exp2(logits - top).astype(BF16))
            mixed.append(dot(jnp.concatenate(expos, axis=1), both, 1, 0))
        mixed = jnp.concatenate(mixed, axis=0)
        share = jnp.where(mine, mixed[:, :width] / mixed[:, width:], 0.0)
        attended.append((gate_ref[row] * share).astype(BF16))
    return attended


def own_heads_kernel(
    head_dim,
    first_head,
    normed_ref,
    bias_ref,
    small_ref,
    win_ref,
    query_ref,
    key_ref,
    value_ref,
    gate_ref,
    out_ref,
    scratch,
    bias_f,
):
    rows, total, width = normed_ref.shape
    scale = LOG2E / math.sqrt(head_dim)
    packed = [dot(normed_ref[row], win_ref[...], 1, 0) for row in range(rows)]
    for row in range(rows):
        query_ref[row] = (packed[row][:, 0:width] * scale).astype(BF16)
        key_ref[row] = packed[row][:, width : 2 * width].astype(BF16)
        value_ref[row] = packed[row][:, 2 * width : 3 * width].astype(BF16)
        gate_ref[row] = sigmoid(packed[row][:, 3 * width : 4 * width])
    attended = attend(
        head_dim, first_head, query_ref, key_ref, value_ref, gate_ref, bias_ref, small_ref, scratch, bias_f
    )
    for row in range(rows):
        out_ref[row] = attended[row]


def other_heads_kernel(
    head_dim,
    first_head,
    query_ref,
    key_ref,
    value_ref,
    gate_ref,
    bias_ref,
    small_ref,
    mid_ref,
    part_ref,
    wout_ref,
    out_ref,
    scratch,
    bias_f,
    result,
    sems,
):
    rows = mid_ref.shape[0]
    attended = attend(
        head_dim, first_head, query_ref, key_ref, value_ref, gate_ref, bias_ref, small_ref, scratch, bias_f
    )
    copies = []
    for row in range(rows):
        update = dot(attended[row] + part_ref[row], wout_ref[...], 1, 0)
        result[row] = (mid_ref[row].astype(F32) + update).astype(BF16)
        copies.append(pltpu.make_async_copy(result.at[row], out_ref.at[row], sems.at[row]))
        copies[row].start()
    for copy in copies:
        copy.wait()


def call(kernel, out_shape, scratch, n_args, scalars=0, limit=VMEM_LIMIT, in_space=pltpu.VMEM, out_space=pltpu.VMEM, cost=None):
    specs = [
        pl.BlockSpec(memory_space=pltpu.SMEM if at < scalars else in_space) for at in range(n_args)
    ]
    return pl.pallas_call(
        kernel,
        in_specs=specs,
        out_specs=jax.tree.map(lambda _: pl.BlockSpec(memory_space=out_space), out_shape),
        out_shape=out_shape,
        scratch_shapes=scratch,
        compiler_params=pltpu.CompilerParams(vmem_limit_bytes=limit),
        cost_estimate=cost,
    )


def exchange(array):
    return lax.all_to_all(array, "dap", 0, 0, tiled=True)


def per_device(
    pair, pair_mask, norm_gains, w_edges, w_tri_gate, w_tri_out, w_attn_in, w_tri_bias, w_attn_out
):
    rows, total, width = pair.shape
    hidden = w_tri_out.shape[0]
    heads = w_tri_bias.shape[1]
    head_dim = width // heads
    own = heads // 2
    devices = total // rows
    lanes = total // 128
    shape = jax.ShapeDtypeStruct
    tall = pltpu.VMEM((lanes, (devices + 1) * TILE, 128), F32)
    square = pltpu.VMEM((lanes, total + TILE, 128), F32)
    short = pltpu.VMEM((lanes // 2, (devices + 1) * TILE, 128), F32)
    inputs = [pair, pair_mask, norm_gains, w_edges]
    kept = [pltpu.VMEM(array.shape, array.dtype) for array in inputs]
    sides = call(
        edges_kernel,
        shape((hidden, TILE, total), BF16),
        [tall] + kept + [pltpu.VMEM((hidden, TILE, total), BF16), pltpu.SemaphoreType.DMA((4 + lanes,))],
        4,
        limit=EDGES_LIMIT,
        in_space=pl.ANY,
        out_space=pl.ANY,
    )(*inputs)
    gate, small = call(
        gate_kernel,
        [shape((rows, total, width), F32), shape((SMALL, total), F32)],
        [],
        5,
        cost=pl.CostEstimate(
            flops=2 * rows * total * width * width,
            bytes_accessed=4 * rows * total * width,
            transcendentals=rows * total * width,
        ),
    )(pair, pair_mask, norm_gains, w_tri_gate, w_tri_bias.T)
    sides = exchange(sides)
    sides, gate, small = lax.optimization_barrier((sides, gate, small))
    product = call(
        product_kernel, shape((devices, TILE, total // 2), BF16), [tall, square, short], 1
    )(sides)
    product = exchange(product)
    like = shape((rows, total, width), BF16)
    wide = shape((rows, total, width), F32)
    mid, mid_normed, bias = call(
        middle_kernel,
        [like, like, shape((devices, TILE, total), BF16)],
        [short, pltpu.VMEM((2 * TILE, total), F32)],
        5,
    )(product, pair, gate, small, w_tri_out)
    mine = exchange(bias)
    swap = [(d, d ^ 1) for d in range(devices)]
    other = lax.ppermute(mine, "dap", swap)
    core = lax.rem(lax.axis_index("dap"), 2)
    mine_first = jnp.reshape(core * own, (1,))
    other_first = jnp.reshape((1 - core) * own, (1,))
    scratch = [tall, pltpu.VMEM((own, lanes, total + TILE, 128), F32)]
    query, key, value, att_gate, part = call(
        functools.partial(own_heads_kernel, head_dim),
        [like, like, like, wide, like],
        scratch,
        5,
        1,
    )(mine_first, mid_normed, mine, small, w_attn_in)
    scratch = scratch + [pltpu.VMEM((rows, total, width), BF16), pltpu.SemaphoreType.DMA((rows,))]
    return call(
        functools.partial(other_heads_kernel, head_dim),
        like,
        scratch,
        10,
        1,
        out_space=pl.ANY,
    )(other_first, query, key, value, att_gate, other, small, mid, part, w_attn_out)


def solution(mesh):
    placed = (P("dap", None, None), P("dap", None), P(), P(), P(), P(), P(), P(), P())
    return jax.shard_map(
        per_device, mesh=mesh, in_specs=placed, out_specs=P("dap", None, None), check_vma=False
    )
```

```python
import functools
import math

import jax
import jax.numpy as jnp
from jax import lax
from jax.experimental import pallas as pl
from jax.experimental.pallas import tpu as pltpu
from jax.sharding import PartitionSpec as P

F32 = jnp.float32
BF16 = jnp.bfloat16
VMEM_LIMIT = 40 * 1024 * 1024
EDGES_LIMIT = 60 * 1024 * 1024
LOG2E = math.log2(math.e)
TILE = 8
MASK_AT, GAIN_AT, BIAS_AT, SMALL = 0, 8, 16, 24


def dot(a, b, ca, cb):
    return lax.dot_general(a, b, (((ca,), (cb,)), ((), ())), preferred_element_type=F32)


def sigmoid(x):
    return 0.5 + 0.5 * jnp.tanh(0.5 * x)


def norm_rows(values, gain, mats):
    size = values.shape[-1]
    centered = dot(values, mats[0:size], 1, 0)
    var = dot((centered * centered).astype(BF16), mats[size : 2 * size], 1, 0)
    return (centered * lax.rsqrt(var + 1e-05) * gain).astype(BF16)


def mats_kernel(out_ref):
    size = out_ref.shape[1]
    row = lax.broadcasted_iota(jnp.int32, (size, size), 0)
    col = lax.broadcasted_iota(jnp.int32, (size, size), 1)
    out_ref[0:size, :] = ((row == col).astype(F32) - 1.0 / size).astype(BF16)
    out_ref[size : 2 * size, :] = jnp.full((size, size), 1.0 / size, BF16)


def put_rows(scratch, start, stride, values):
    for lane in range(values.shape[1] // 128):
        scratch[lane, pl.ds(start, values.shape[0], stride=stride), :] = values[:, lane * 128 : (lane + 1) * 128]


def get_rows(scratch, start, size, stride):
    return jnp.concatenate(
        [scratch[lane, pl.ds(start, size, stride=stride), :] for lane in range(scratch.shape[0])], axis=1
    )


def spill(scratch, values):
    for lane in range(scratch.shape[0]):
        part = values[:, :, lane * 128 : (lane + 1) * 128].astype(F32)
        scratch[lane, 0 : values.shape[0] * TILE, :] = part.reshape(values.shape[0] * TILE, 128)


def fill(out_ref, scratch):
    for lane in range(scratch.shape[0]):
        part = scratch[lane, 0 : out_ref.shape[0] * TILE, :].reshape(out_ref.shape[0], TILE, 128)
        out_ref[:, :, lane * 128 : (lane + 1) * 128] = part.astype(BF16)


def edges_kernel(
    mats_ref, pair_ref, mask_ref, gains_ref, w_ref, wg_ref, wb_ref, out_ref, gate_ref, small_ref, scratch
):
    rows, total = mask_ref.shape
    hidden = out_ref.shape[0]
    width = gains_ref.shape[1]
    small_ref[MASK_AT : MASK_AT + rows, :] = (1000000000.0 * LOG2E) * (mask_ref[...].astype(F32) - 1.0)
    small_ref[GAIN_AT : GAIN_AT + 3, 0:width] = gains_ref[...]
    small_ref[BIAS_AT : BIAS_AT + wb_ref.shape[0], 0:width] = wb_ref[...].astype(F32)
    mats = mats_ref[...]
    normed = [norm_rows(pair_ref[row], gains_ref[0:1, :], mats) for row in range(rows)]
    edges = [dot(w_ref[...], normed[row], 0, 1) for row in range(rows)]
    for row in range(rows):
        gate_ref[row] = sigmoid(dot(normed[row], wg_ref[...], 1, 0))
    for row in range(rows):
        mask = mask_ref[row : row + 1, :].astype(F32)
        for side in range(2):
            gate = edges[row][2 * side * hidden : (2 * side + 1) * hidden]
            value = edges[row][(2 * side + 1) * hidden : (2 * side + 2) * hidden]
            put_rows(scratch, side * rows + row, TILE, mask * sigmoid(gate) * value)
    fill(out_ref, scratch)


def product_kernel(sides_ref, out_ref, scratch, right_ref, prod_ref):
    devices, _, total = sides_ref.shape
    rows = total // devices
    half = total // 2
    spill(scratch, sides_ref[...])
    for row in range(rows):
        put_rows(right_ref, row, rows, get_rows(scratch, rows + row, devices, TILE))
    right = jnp.concatenate([right_ref[lane, 0:total, :] for lane in range(total // 128)], axis=1).astype(BF16)
    left = [get_rows(scratch, row, devices, TILE).astype(BF16) for row in range(rows)]
    product = dot(jnp.concatenate(left, axis=0), right, 1, 1)
    for row in range(rows):
        for part in range(2):
            put_rows(prod_ref, 2 * row + part, TILE, product[row * devices : (row + 1) * devices, part * half : (part + 1) * half])
    fill(out_ref, prod_ref)


def middle_kernel(
    mats_ref,
    prod_ref,
    pair_ref,
    gate_ref,
    small_ref,
    wo_ref,
    mid_ref,
    normed_ref,
    bias_ref,
    scratch,
    bias_f,
):
    rows, total, width = pair_ref.shape
    heads = 2 * TILE // rows
    devices = bias_ref.shape[0]
    spill(scratch, prod_ref[...])
    gain = small_ref[GAIN_AT + 1 : GAIN_AT + 2, 0:width].T
    wb = small_ref[BIAS_AT : BIAS_AT + heads, 0:width].astype(BF16)
    prod_normed = []
    for row in range(rows):
        prod = jnp.concatenate(
            [get_rows(scratch, 2 * row + part, width, TILE) for part in range(2)], axis=1
        )
        mean = jnp.mean(prod, axis=0, keepdims=True)
        centered = prod - mean
        var = jnp.mean(centered * centered, axis=0, keepdims=True)
        prod_normed.append((centered * lax.rsqrt(var + 1e-05) * gain).astype(BF16))
    update = [dot(prod_normed[row], wo_ref[...], 0, 0) for row in range(rows)]
    mid = [(pair_ref[row].astype(F32) + gate_ref[row] * update[row]).astype(BF16) for row in range(rows)]
    mid_normed = []
    for row in range(rows):
        mid_ref[row] = mid[row]
        mid_normed.append(norm_rows(mid[row], small_ref[GAIN_AT + 2 : GAIN_AT + 3, 0:width], mats_ref[...]))
        normed_ref[row] = mid_normed[row]
    bias = [dot(wb, mid_normed[row], 1, 1) for row in range(rows)]
    for row in range(rows):
        for head in range(heads):
            bias_f[head * rows + row : head * rows + row + 1, :] = bias[row][head : head + 1, :]
    for part in range(2):
        block = bias_f[part * TILE : (part + 1) * TILE, :].astype(BF16)
        for pair_of in range(devices // 2):
            bias_ref[2 * pair_of + part] = block


def attend(head_dim, first_head, query_ref, key_ref, value_ref, gate_ref, bias_ref, small_ref, scratch, bias_f):
    rows, total, width = value_ref.shape
    devices = bias_ref.shape[0]
    own = TILE // rows
    spill(scratch, bias_ref[...])
    for head in range(own):
        for row in range(rows):
            values = get_rows(scratch, head * rows + row, devices, TILE) * LOG2E
            put_rows(bias_f.at[head], row, rows, values)
    base = first_head[0]
    lane_head = lax.broadcasted_iota(jnp.int32, (1, width), 1) // head_dim
    mine = (lane_head >= base) & (lane_head < base + own)
    step = total // 4
    picks = [(lane_head == base + head).astype(BF16) for head in range(own)]
    attended = []
    for row in range(rows):
        value = value_ref[row]
        both = jnp.concatenate(
            [jnp.concatenate([value * pick, jnp.broadcast_to(pick, value.shape)], axis=1) for pick in picks],
            axis=0,
        )
        mixed = []
        for at in range(0, total, step):
            here = slice(at, at + step)
            expos = []
            for head in range(own):
                bias = jnp.concatenate([bias_f[head, lane, here] for lane in range(total // 128)], axis=1)
                logits = dot(query_ref[row, here] * picks[head], key_ref[row], 1, 1) + bias
                logits = logits + small_ref[MASK_AT + row : MASK_AT + row + 1, :]
                top = jnp.max(logits, axis=-1, keepdims=True)
                expos.append(jnp.exp2(logits - top).astype(BF16))
            mixed.append(dot(jnp.concatenate(expos, axis=1), both, 1, 0))
        mixed = jnp.concatenate(mixed, axis=0)
        share = jnp.where(mine, mixed[:, :width] / mixed[:, width:], 0.0)
        attended.append((gate_ref[row] * share).astype(BF16))
    return attended


def own_heads_kernel(
    head_dim,
    first_head,
    normed_ref,
    bias_ref,
    small_ref,
    win_ref,
    query_ref,
    key_ref,
    value_ref,
    gate_ref,
    out_ref,
    scratch,
    bias_f,
):
    rows, total, width = normed_ref.shape
    scale = LOG2E / math.sqrt(head_dim)
    packed = [dot(normed_ref[row], win_ref[...], 1, 0) for row in range(rows)]
    for row in range(rows):
        query_ref[row] = (packed[row][:, 0:width] * scale).astype(BF16)
        key_ref[row] = packed[row][:, width : 2 * width].astype(BF16)
        value_ref[row] = packed[row][:, 2 * width : 3 * width].astype(BF16)
        gate_ref[row] = sigmoid(packed[row][:, 3 * width : 4 * width])
    attended = attend(
        head_dim, first_head, query_ref, key_ref, value_ref, gate_ref, bias_ref, small_ref, scratch, bias_f
    )
    for row in range(rows):
        out_ref[row] = attended[row]


def other_heads_kernel(
    head_dim,
    first_head,
    query_ref,
    key_ref,
    value_ref,
    gate_ref,
    bias_ref,
    small_ref,
    mid_ref,
    part_ref,
    wout_ref,
    out_ref,
    scratch,
    bias_f,
    result,
    sems,
):
    rows = mid_ref.shape[0]
    attended = attend(
        head_dim, first_head, query_ref, key_ref, value_ref, gate_ref, bias_ref, small_ref, scratch, bias_f
    )
    copies = []
    for row in range(rows):
        update = dot(attended[row] + part_ref[row], wout_ref[...], 1, 0)
        result[row] = (mid_ref[row].astype(F32) + update).astype(BF16)
        copies.append(pltpu.make_async_copy(result.at[row], out_ref.at[row], sems.at[row]))
        copies[row].start()
    for copy in copies:
        copy.wait()


def call(kernel, out_shape, scratch, n_args, scalars=0, limit=VMEM_LIMIT, in_space=pltpu.VMEM, out_space=pltpu.VMEM, cost=None):
    specs = [
        pl.BlockSpec(memory_space=pltpu.SMEM if at < scalars else in_space) for at in range(n_args)
    ]
    return pl.pallas_call(
        kernel,
        in_specs=specs,
        out_specs=jax.tree.map(lambda _: pl.BlockSpec(memory_space=out_space), out_shape),
        out_shape=out_shape,
        scratch_shapes=scratch,
        compiler_params=pltpu.CompilerParams(vmem_limit_bytes=limit),
        cost_estimate=cost,
    )


def exchange(array):
    return lax.all_to_all(array, "dap", 0, 0, tiled=True)


def per_device(
    pair, pair_mask, norm_gains, w_edges, w_tri_gate, w_tri_out, w_attn_in, w_tri_bias, w_attn_out
):
    rows, total, width = pair.shape
    hidden = w_tri_out.shape[0]
    heads = w_tri_bias.shape[1]
    head_dim = width // heads
    own = heads // 2
    devices = total // rows
    lanes = total // 128
    shape = jax.ShapeDtypeStruct
    tall = pltpu.VMEM((lanes, (devices + 1) * TILE, 128), F32)
    square = pltpu.VMEM((lanes, total + TILE, 128), F32)
    short = pltpu.VMEM((lanes // 2, (devices + 1) * TILE, 128), F32)
    mats = call(
        mats_kernel,
        shape((2 * width, width), BF16),
        [],
        0,
        cost=pl.CostEstimate(flops=1 << 31, bytes_accessed=8 << 20, transcendentals=0),
    )()
    sides, gate, small = call(
        edges_kernel,
        [
            shape((hidden, TILE, total), BF16),
            shape((rows, total, width), F32),
            shape((SMALL, total), F32),
        ],
        [tall],
        7,
    )(mats, pair, pair_mask, norm_gains, w_edges, w_tri_gate, w_tri_bias.T)
    sides = exchange(sides)
    product = call(
        product_kernel, shape((devices, TILE, total // 2), BF16), [tall, square, short], 1
    )(sides)
    product = exchange(product)
    like = shape((rows, total, width), BF16)
    wide = shape((rows, total, width), F32)
    mid, mid_normed, bias = call(
        middle_kernel,
        [like, like, shape((devices, TILE, total), BF16)],
        [short, pltpu.VMEM((2 * TILE, total), F32)],
        6,
    )(mats, product, pair, gate, small, w_tri_out)
    mine = exchange(bias)
    swap = [(d, d ^ 1) for d in range(devices)]
    other = lax.ppermute(mine, "dap", swap)
    core = lax.rem(lax.axis_index("dap"), 2)
    mine_first = jnp.reshape(core * own, (1,))
    other_first = jnp.reshape((1 - core) * own, (1,))
    scratch = [tall, pltpu.VMEM((own, lanes, total + TILE, 128), F32)]
    query, key, value, att_gate, part = call(
        functools.partial(own_heads_kernel, head_dim),
        [like, like, like, wide, like],
        scratch,
        5,
        1,
    )(mine_first, mid_normed, mine, small, w_attn_in)
    scratch = scratch + [pltpu.VMEM((rows, total, width), BF16), pltpu.SemaphoreType.DMA((rows,))]
    return call(
        functools.partial(other_heads_kernel, head_dim),
        like,
        scratch,
        10,
        1,
        out_space=pl.ANY,
    )(other_first, query, key, value, att_gate, other, small, mid, part, w_attn_out)


def solution(mesh):
    placed = (P("dap", None, None), P("dap", None), P(), P(), P(), P(), P(), P(), P())
    return jax.shard_map(
        per_device, mesh=mesh, in_specs=placed, out_specs=P("dap", None, None), check_vma=False
    )
```

```python
import functools
import math

import jax
import jax.numpy as jnp
from jax import lax
from jax.experimental import pallas as pl
from jax.experimental.pallas import tpu as pltpu
from jax.sharding import PartitionSpec as P

F32 = jnp.float32
BF16 = jnp.bfloat16
VMEM_LIMIT = 40 * 1024 * 1024
EDGES_LIMIT = 60 * 1024 * 1024
LOG2E = math.log2(math.e)
TILE = 8
MASK_AT, GAIN_AT, BIAS_AT, SMALL = 0, 8, 16, 24


def dot(a, b, ca, cb):
    return lax.dot_general(a, b, (((ca,), (cb,)), ((), ())), preferred_element_type=F32)


def sigmoid(x):
    return 0.5 + 0.5 * jnp.tanh(0.5 * x)


def norm_rows(values, gain, mats):
    size = values.shape[-1]
    centered = dot(values, mats[0:size], 1, 0)
    var = dot((centered * centered).astype(BF16), mats[size : 2 * size], 1, 0)
    return (centered * lax.rsqrt(var + 1e-05) * gain).astype(BF16)


def mats_kernel(out_ref):
    size = out_ref.shape[1]
    row = lax.broadcasted_iota(jnp.int32, (size, size), 0)
    col = lax.broadcasted_iota(jnp.int32, (size, size), 1)
    out_ref[0:size, :] = ((row == col).astype(F32) - 1.0 / size).astype(BF16)
    out_ref[size : 2 * size, :] = jnp.full((size, size), 1.0 / size, BF16)


def put_rows(scratch, start, stride, values):
    for lane in range(values.shape[1] // 128):
        scratch[lane, pl.ds(start, values.shape[0], stride=stride), :] = values[:, lane * 128 : (lane + 1) * 128]


def get_rows(scratch, start, size, stride):
    return jnp.concatenate(
        [scratch[lane, pl.ds(start, size, stride=stride), :] for lane in range(scratch.shape[0])], axis=1
    )


def spill(scratch, values):
    for lane in range(scratch.shape[0]):
        part = values[:, :, lane * 128 : (lane + 1) * 128].astype(F32)
        scratch[lane, 0 : values.shape[0] * TILE, :] = part.reshape(values.shape[0] * TILE, 128)


def fill(out_ref, scratch):
    for lane in range(scratch.shape[0]):
        part = scratch[lane, 0 : out_ref.shape[0] * TILE, :].reshape(out_ref.shape[0], TILE, 128)
        out_ref[:, :, lane * 128 : (lane + 1) * 128] = part.astype(BF16)


def edges_kernel(
    mats_ref, pair_ref, mask_ref, gains_ref, w_ref, wg_ref, wb_ref, out_ref, gate_ref, small_ref, scratch
):
    rows, total = mask_ref.shape
    hidden = out_ref.shape[0]
    width = gains_ref.shape[1]
    small_ref[MASK_AT : MASK_AT + rows, :] = (1000000000.0 * LOG2E) * (mask_ref[...].astype(F32) - 1.0)
    small_ref[GAIN_AT : GAIN_AT + 3, 0:width] = gains_ref[...]
    small_ref[BIAS_AT : BIAS_AT + wb_ref.shape[0], 0:width] = wb_ref[...].astype(F32)
    mats = mats_ref[...]
    normed = [norm_rows(pair_ref[row], gains_ref[0:1, :], mats) for row in range(rows)]
    edges = [dot(w_ref[...], normed[row], 0, 1) for row in range(rows)]
    for row in range(rows):
        gate_ref[row] = sigmoid(dot(normed[row], wg_ref[...], 1, 0))
    for row in range(rows):
        mask = mask_ref[row : row + 1, :].astype(F32)
        for side in range(2):
            gate = edges[row][2 * side * hidden : (2 * side + 1) * hidden]
            value = edges[row][(2 * side + 1) * hidden : (2 * side + 2) * hidden]
            put_rows(scratch, side * rows + row, TILE, mask * sigmoid(gate) * value)
    fill(out_ref, scratch)


def product_kernel(sides_ref, out_ref, scratch, right_ref, prod_ref):
    devices, _, total = sides_ref.shape
    rows = total // devices
    half = total // 2
    spill(scratch, sides_ref[...])
    for row in range(rows):
        put_rows(right_ref, row, rows, get_rows(scratch, rows + row, devices, TILE))
    right = jnp.concatenate([right_ref[lane, 0:total, :] for lane in range(total // 128)], axis=1).astype(BF16)
    left = [get_rows(scratch, row, devices, TILE).astype(BF16) for row in range(rows)]
    product = dot(jnp.concatenate(left, axis=0), right, 1, 1)
    for row in range(rows):
        for part in range(2):
            put_rows(prod_ref, 2 * row + part, TILE, product[row * devices : (row + 1) * devices, part * half : (part + 1) * half])
    fill(out_ref, prod_ref)


def middle_kernel(
    mats_ref,
    prod_ref,
    pair_ref,
    gate_ref,
    small_ref,
    wo_ref,
    mid_ref,
    normed_ref,
    bias_ref,
    scratch,
    bias_f,
):
    rows, total, width = pair_ref.shape
    heads = 2 * TILE // rows
    devices = bias_ref.shape[0]
    spill(scratch, prod_ref[...])
    gain = small_ref[GAIN_AT + 1 : GAIN_AT + 2, 0:width].T
    wb = small_ref[BIAS_AT : BIAS_AT + heads, 0:width].astype(BF16)
    prod_normed = []
    for row in range(rows):
        prod = jnp.concatenate(
            [get_rows(scratch, 2 * row + part, width, TILE) for part in range(2)], axis=1
        )
        mean = jnp.mean(prod, axis=0, keepdims=True)
        centered = prod - mean
        var = jnp.mean(centered * centered, axis=0, keepdims=True)
        prod_normed.append((centered * lax.rsqrt(var + 1e-05) * gain).astype(BF16))
    update = [dot(prod_normed[row], wo_ref[...], 0, 0) for row in range(rows)]
    mid = [(pair_ref[row].astype(F32) + gate_ref[row] * update[row]).astype(BF16) for row in range(rows)]
    mid_normed = []
    for row in range(rows):
        mid_ref[row] = mid[row]
        mid_normed.append(norm_rows(mid[row], small_ref[GAIN_AT + 2 : GAIN_AT + 3, 0:width], mats_ref[...]))
        normed_ref[row] = mid_normed[row]
    bias = [dot(wb, mid_normed[row], 1, 1) * LOG2E for row in range(rows)]
    for row in range(rows):
        for head in range(heads):
            bias_f[head * rows + row : head * rows + row + 1, :] = bias[row][head : head + 1, :]
    for part in range(2):
        block = bias_f[part * TILE : (part + 1) * TILE, :].astype(BF16)
        for pair_of in range(devices // 2):
            bias_ref[2 * pair_of + part] = block


def attend(head_dim, first_head, query_ref, key_ref, value_ref, gate_ref, bias_ref, small_ref, scratch, bias_f):
    rows, total, width = value_ref.shape
    devices = bias_ref.shape[0]
    own = TILE // rows
    spill(scratch, bias_ref[...])
    for head in range(own):
        for row in range(rows):
            values = get_rows(scratch, head * rows + row, devices, TILE)
            put_rows(bias_f.at[head], row, rows, values)
    base = first_head[0]
    lane_head = lax.broadcasted_iota(jnp.int32, (1, width), 1) // head_dim
    mine = (lane_head >= base) & (lane_head < base + own)
    step = total // 4
    picks = [(lane_head == base + head).astype(BF16) for head in range(own)]
    attended = []
    for row in range(rows):
        value = value_ref[row]
        both = jnp.concatenate(
            [jnp.concatenate([value * pick, jnp.broadcast_to(pick, value.shape)], axis=1) for pick in picks],
            axis=0,
        )
        mixed = []
        for at in range(0, total, step):
            here = slice(at, at + step)
            expos = []
            for head in range(own):
                bias = jnp.concatenate([bias_f[head, lane, here] for lane in range(total // 128)], axis=1)
                logits = dot(query_ref[row, here] * picks[head], key_ref[row], 1, 1) + bias
                logits = logits + small_ref[MASK_AT + row : MASK_AT + row + 1, :]
                top = jnp.max(logits, axis=-1, keepdims=True)
                expos.append(jnp.exp2(logits - top).astype(BF16))
            mixed.append(dot(jnp.concatenate(expos, axis=1), both, 1, 0))
        mixed = jnp.concatenate(mixed, axis=0)
        share = jnp.where(mine, mixed[:, :width] / mixed[:, width:], 0.0)
        attended.append((gate_ref[row] * share).astype(BF16))
    return attended


def own_heads_kernel(
    head_dim,
    first_head,
    normed_ref,
    bias_ref,
    small_ref,
    win_ref,
    query_ref,
    key_ref,
    value_ref,
    gate_ref,
    out_ref,
    scratch,
    bias_f,
):
    rows, total, width = normed_ref.shape
    scale = LOG2E / math.sqrt(head_dim)
    packed = [dot(normed_ref[row], win_ref[...], 1, 0) for row in range(rows)]
    for row in range(rows):
        query_ref[row] = (packed[row][:, 0:width] * scale).astype(BF16)
        key_ref[row] = packed[row][:, width : 2 * width].astype(BF16)
        value_ref[row] = packed[row][:, 2 * width : 3 * width].astype(BF16)
        gate_ref[row] = sigmoid(packed[row][:, 3 * width : 4 * width])
    attended = attend(
        head_dim, first_head, query_ref, key_ref, value_ref, gate_ref, bias_ref, small_ref, scratch, bias_f
    )
    for row in range(rows):
        out_ref[row] = attended[row]


def other_heads_kernel(
    head_dim,
    first_head,
    query_ref,
    key_ref,
    value_ref,
    gate_ref,
    bias_ref,
    small_ref,
    mid_ref,
    part_ref,
    wout_ref,
    out_ref,
    scratch,
    bias_f,
    result,
    sems,
):
    rows = mid_ref.shape[0]
    attended = attend(
        head_dim, first_head, query_ref, key_ref, value_ref, gate_ref, bias_ref, small_ref, scratch, bias_f
    )
    copies = []
    for row in range(rows):
        update = dot(attended[row] + part_ref[row], wout_ref[...], 1, 0)
        result[row] = (mid_ref[row].astype(F32) + update).astype(BF16)
        copies.append(pltpu.make_async_copy(result.at[row], out_ref.at[row], sems.at[row]))
        copies[row].start()
    for copy in copies:
        copy.wait()


def call(kernel, out_shape, scratch, n_args, scalars=0, limit=VMEM_LIMIT, in_space=pltpu.VMEM, out_space=pltpu.VMEM, cost=None):
    specs = [
        pl.BlockSpec(memory_space=pltpu.SMEM if at < scalars else in_space) for at in range(n_args)
    ]
    return pl.pallas_call(
        kernel,
        in_specs=specs,
        out_specs=jax.tree.map(lambda _: pl.BlockSpec(memory_space=out_space), out_shape),
        out_shape=out_shape,
        scratch_shapes=scratch,
        compiler_params=pltpu.CompilerParams(vmem_limit_bytes=limit),
        cost_estimate=cost,
    )


def exchange(array):
    return lax.all_to_all(array, "dap", 0, 0, tiled=True)


def per_device(
    pair, pair_mask, norm_gains, w_edges, w_tri_gate, w_tri_out, w_attn_in, w_tri_bias, w_attn_out
):
    rows, total, width = pair.shape
    hidden = w_tri_out.shape[0]
    heads = w_tri_bias.shape[1]
    head_dim = width // heads
    own = heads // 2
    devices = total // rows
    lanes = total // 128
    shape = jax.ShapeDtypeStruct
    tall = pltpu.VMEM((lanes, (devices + 1) * TILE, 128), F32)
    square = pltpu.VMEM((lanes, total + TILE, 128), F32)
    short = pltpu.VMEM((lanes // 2, (devices + 1) * TILE, 128), F32)
    mats = call(
        mats_kernel,
        shape((2 * width, width), BF16),
        [],
        0,
        cost=pl.CostEstimate(flops=1 << 31, bytes_accessed=8 << 20, transcendentals=0),
    )()
    sides, gate, small = call(
        edges_kernel,
        [
            shape((hidden, TILE, total), BF16),
            shape((rows, total, width), F32),
            shape((SMALL, total), F32),
        ],
        [tall],
        7,
    )(mats, pair, pair_mask, norm_gains, w_edges, w_tri_gate, w_tri_bias.T)
    sides = exchange(sides)
    product = call(
        product_kernel, shape((devices, TILE, total // 2), BF16), [tall, square, short], 1
    )(sides)
    product = exchange(product)
    like = shape((rows, total, width), BF16)
    wide = shape((rows, total, width), F32)
    mid, mid_normed, bias = call(
        middle_kernel,
        [like, like, shape((devices, TILE, total), BF16)],
        [short, pltpu.VMEM((2 * TILE, total), F32)],
        6,
    )(mats, product, pair, gate, small, w_tri_out)
    mine = exchange(bias)
    swap = [(d, d ^ 1) for d in range(devices)]
    other = lax.ppermute(mine, "dap", swap)
    core = lax.rem(lax.axis_index("dap"), 2)
    mine_first = jnp.reshape(core * own, (1,))
    other_first = jnp.reshape((1 - core) * own, (1,))
    scratch = [tall, pltpu.VMEM((own, lanes, total + TILE, 128), F32)]
    query, key, value, att_gate, part = call(
        functools.partial(own_heads_kernel, head_dim),
        [like, like, like, wide, like],
        scratch,
        5,
        1,
    )(mine_first, mid_normed, mine, small, w_attn_in)
    scratch = scratch + [pltpu.VMEM((rows, total, width), BF16), pltpu.SemaphoreType.DMA((rows,))]
    return call(
        functools.partial(other_heads_kernel, head_dim),
        like,
        scratch,
        10,
        1,
        out_space=pl.ANY,
    )(other_first, query, key, value, att_gate, other, small, mid, part, w_attn_out)


def solution(mesh):
    placed = (P("dap", None, None), P("dap", None), P(), P(), P(), P(), P(), P(), P())
    return jax.shard_map(
        per_device, mesh=mesh, in_specs=placed, out_specs=P("dap", None, None), check_vma=False
    )
```
